32 devices in a mesh: gx: 4 (over z), gy: 8 (over y, x, core).
Axes of the slice: x: 2, y: 2, z: 4, core: 2. Of those that a mesh axis runs over, the one named last changes fastest.
Arguments:
- center_points: float32 [3, 8192], P(None, ('gx', 'gy')), may hold values from 0 to 1
- displacements: float32 [3, 8192], P(None, ('gx', 'gy')), may hold values from -24 to 24
- edge_points: float32 [3, 32768], P(None, ('gx', 'gy')), may hold values from 0 to 1
- send_list: int32 [32, 8, 6], P(('gx', 'gy')), may hold values from -1 to 15, as said below
- block_tiles: int32 [128, 12], P(('gx', 'gy')), may hold values from 0 to 47, as said below
- block_count: int32 [32], P(('gx', 'gy')), may hold values from 1 to 4, as said below
Outputs:
- coefficients: float32 [3, 8192], P(None, ('gx', 'gy'))
- block_motion: float32 [128, 3, 64, 4096], P(('gx', 'gy'))
The draws below stay inside these ranges and needn't reach their ends.
Inputs may be any that keep to these rules, and one draw needn't show every extreme that they name: `send_list`: A zone is the 8 devices that share a gx index. Entry [s, r, c] names the local edge that device s sends to device r of its zone in position c, or -1 where that position carries nothing. Every position that a live block slot names carries an edge. `block_tiles`: the entry for a block slot and edge is the position s * 6 + c, in the tiles that reach the block's device, of the tile sent by device s of its zone in position c; the 48 entries of one device are all distinct, so a device with 4 live blocks receives 6 tiles from every device of its zone. `block_count`: the live slots of a device are its first ones; in every zone some device holds 4 blocks.
All inputs are finite; a program needn't handle non-finite values.
Results may differ from the reference program's by a relative error of at most 0.0003.
Values sent between devices are 32-bit elements; how exact they have to be, the bound alone decides.
No kernel may reach another device: no remote copies, remote signals or barrier semaphores. Data moves between devices by JAX's collectives and lax.ppermute only.
A program may use at most 128 MiB of HBM per device.

```python
import jax
import jax.numpy as jnp
from jax import lax

NC = 8192
S = 64
ITERS = 3
SLOTS = 4
EDGE_DEV = 16
CAP = 6
N_GX = 4
N_GY = 8


def layout_tables(key):
    zones = N_GX
    group_size = N_GY
    devices = N_GX * N_GY
    places = SLOTS * 12
    base_key = jax.random.fold_in(key, 4242)
    key_count, key_full, key_perm, key_edge = jax.random.split(base_key, 4)
    counts = jax.random.randint(key_count, (zones, group_size), 1, SLOTS + 1)
    fullest = jax.random.randint(key_full, (zones, 1), 0, group_size)
    counts = jnp.where(jnp.arange(group_size)[None, :] == fullest, SLOTS, counts).reshape(devices).astype(jnp.int32)
    orders = jax.vmap(lambda sub_key: jax.random.permutation(sub_key, places))(jax.random.split(key_perm, devices)).astype(jnp.int32)
    edge_ids = jax.random.randint(key_edge, (devices, places), 0, EDGE_DEV).astype(jnp.int32)
    alive_tile = jnp.arange(places)[None, :] // 12 < counts[:, None]
    inverse = jnp.argsort(orders, axis=1)
    wanted = jnp.where(jnp.take_along_axis(alive_tile, inverse, 1), jnp.take_along_axis(edge_ids, inverse, 1), -1)
    sends = wanted.reshape(zones, group_size, group_size, CAP).transpose(0, 2, 1, 3).reshape(devices, group_size, CAP)
    tiles_table = orders.reshape(devices * SLOTS, 12)
    return (counts, sends.astype(jnp.int32), tiles_table)


def draw_send_list(key, part):
    return layout_tables(key)[1]


def draw_block_tiles(key, part):
    return layout_tables(key)[2]


def draw_block_count(key, part):
    return layout_tables(key)[0]


def draw_displacements(key, part):
    base_key = jax.random.fold_in(key, 1717)
    key_base = jax.random.fold_in(base_key, 0)
    ramp = 1.0 + 2.0 * jnp.arange(NC).astype(jnp.float32) / (NC - 1)
    values = jnp.clip(jax.random.normal(key_base, (3, NC), jnp.float32), -8.0, 8.0) * ramp[None, :]
    return jnp.clip(values, -24.0, 24.0)


def steps_of(stream_key, shape, shards, low, largest):
    def one(axis_at, shards_of):
        steps = jax.random.uniform(jax.random.fold_in(jax.random.fold_in(stream_key, 6), axis_at), (shards_of,), jnp.float32, low / len(shards), largest / len(shards))
        return jnp.repeat(jnp.exp(steps), shape[axis_at] // shards_of).reshape((-1,) + (1,) * (len(shape) - axis_at - 1))

    loudness = one(*shards[0])
    for cut in shards[1:]:
        loudness = loudness * one(*cut)
    return loudness


def setup_inputs(seed: int = 0) -> dict:
    arg_keys = jax.random.split(jax.random.key(seed), 7)
    return {
        "center_points": jnp.clip(1.0 * jax.random.uniform(arg_keys[0], (3, NC), jnp.float32) ** steps_of(arg_keys[0], (3, NC), ((1, 32),), -0.2, 0.2), 0.0, 1.0),
        "displacements": draw_displacements(jax.random.fold_in(arg_keys[6], 71), 0),
        "edge_points": jnp.clip(1.0 * jax.random.uniform(arg_keys[2], (3, N_GX * N_GY * EDGE_DEV * S), jnp.float32) ** steps_of(arg_keys[2], (3, N_GX * N_GY * EDGE_DEV * S), ((1, 32),), -0.2, 0.2), 0.0, 1.0),
        "send_list": draw_send_list(jax.random.fold_in(arg_keys[6], 71), 0),
        "block_tiles": draw_block_tiles(jax.random.fold_in(arg_keys[6], 71), 0),
        "block_count": draw_block_count(jax.random.fold_in(arg_keys[6], 71), 0),
    }


RADIUS = 0.25
SHIFT = 0.1
HIGHEST_PREC = lax.Precision.HIGHEST

def pair_distance(left_points, right_points):
    squared = (left_points[0][:, None] - right_points[0][None, :]) ** 2
    squared = squared + (left_points[1][:, None] - right_points[1][None, :]) ** 2
    squared = squared + (left_points[2][:, None] - right_points[2][None, :]) ** 2
    return squared

def wendland(squared):
    radial = jnp.sqrt(squared) / RADIUS
    remain = jnp.maximum(1.0 - radial, 0.0)
    return remain ** 4 * (4.0 * radial + 1.0)

def transfinite(edge_tiles):
    extent = edge_tiles.shape[2]
    fraction = jnp.arange(extent).astype(jnp.float32) / (extent - 1)
    blends = jnp.stack([1.0 - fraction, fraction])
    pair_weight = (blends[None, :, :, None] * blends[:, None, None, :]).reshape(4, extent, extent)
    first_dir = edge_tiles[:, 0:4]
    second_dir = edge_tiles[:, 4:8]
    third_dir = edge_tiles[:, 8:12]
    straight = blends[0][None, None, :] * first_dir[:, :, 0:1] + blends[1][None, None, :] * first_dir[:, :, extent - 1:extent]
    result = jnp.einsum('cei,ejk->cijk', first_dir - 2.0 * straight, pair_weight, precision=HIGHEST_PREC)
    result = result + jnp.einsum('cej,eik->cijk', second_dir, pair_weight, precision=HIGHEST_PREC)
    result = result + jnp.einsum('cek,eij->cijk', third_dir, pair_weight, precision=HIGHEST_PREC)
    return result.reshape(3, extent, extent * extent)

def conjugate(right_side, matvec, global_sum):
    norm_start = global_sum(lax.optimization_barrier(jnp.sum(right_side * right_side, axis=1, keepdims=True)))

    def cg_turn(iteration, cg_state):
        iterate, remain, search, norm_now = cg_state
        applied = matvec(search)
        step_size = norm_now / global_sum(lax.optimization_barrier(jnp.sum(search * applied, axis=1, keepdims=True)))
        iterate = iterate + step_size * search
        remain = remain - step_size * applied
        norm_next = global_sum(lax.optimization_barrier(jnp.sum(remain * remain, axis=1, keepdims=True)))
        search = remain + norm_next / norm_now * search
        return (iterate, remain, search, norm_next)
    cg_state = lax.fori_loop(0, ITERS, cg_turn, (jnp.zeros_like(right_side), right_side, right_side, norm_start))
    return cg_state[0]

def reference(center_points, displacements, edge_points, send_list, block_tiles, block_count):
    kernel = wendland(pair_distance(center_points, center_points))

    def matvec(search):
        return jnp.dot(search, kernel, precision=HIGHEST_PREC) + SHIFT * search

    def global_sum(partial_value):
        return partial_value
    coefficients = conjugate(displacements, matvec, global_sum)
    devices = N_GX * N_GY
    owned_points = edge_points.reshape(3, devices, EDGE_DEV * S).transpose(1, 0, 2)

    def evaluate(points):
        weights = wendland(pair_distance(points, center_points))
        return jnp.dot(coefficients, weights.T, precision=HIGHEST_PREC)
    motion = lax.map(evaluate, owned_points).reshape(devices, 3, EDGE_DEV, S)
    holder = (jnp.arange(devices * SLOTS) // SLOTS).astype(jnp.int32)
    source = holder[:, None] // N_GY * N_GY + block_tiles // CAP
    receiver = (holder[:, None] % N_GY).astype(jnp.int32)
    column = block_tiles % CAP
    local_edge = jnp.maximum(send_list[source, receiver, column], 0)
    gathered = motion[source, :, local_edge, :].transpose(0, 2, 1, 3)
    alive_slot = jnp.arange(devices * SLOTS).astype(jnp.int32) % SLOTS < block_count[holder]

    def fill_block(element):
        edge_tiles, is_alive = element
        return jnp.where(is_alive, transfinite(edge_tiles), 0.0)
    block_motion = lax.map(fill_block, (gathered, alive_slot))
    return (coefficients, block_motion)
```

```python
import functools

import jax
import jax.numpy as jnp
from jax import lax
from jax.experimental import pallas as pl
from jax.experimental.pallas import tpu as pltpu
from jax.sharding import PartitionSpec as P

S = 64
SHIFT = 0.1
INV_RADIUS = 4.0
TINY = 1e-12
BOTH = ("gx", "gy")
F32, BF16 = jnp.float32, jnp.bfloat16
VMEM = pl.BlockSpec(memory_space=pltpu.VMEM)
SMEM = pl.BlockSpec(memory_space=pltpu.SMEM)
PLAIN = (((1,), (0,)), ((), ()))
LEFT_T = (((0,), (0,)), ((), ()))


def dot(left, right, dims=PLAIN):
    return lax.dot_general(left, right, dims, preferred_element_type=F32)


def split2(value):
    high = value.astype(BF16)
    return high, (value - high.astype(F32)).astype(BF16)


def split3(value):
    high = value.astype(BF16).astype(F32)
    rest = value - high
    middle = rest.astype(BF16).astype(F32)
    return high, middle, rest - middle


def features(points, is_left):
    row = lax.broadcasted_iota(jnp.int32, points.shape, 0)
    is_point = (row >= 4) & (row < 7)
    scaled = jnp.where(is_point, (points - 0.5) * INV_RADIUS, 0.0)
    norm = jnp.sum(scaled * scaled, axis=0, keepdims=True)
    own_row, other_row = (0, 1) if is_left else (1, 0)
    if is_left:
        scaled = -2.0 * scaled
    high, middle, low = split3(scaled)

    def with_norm(part, norm_part):
        return jnp.where(row == own_row, norm_part, jnp.where(row == other_row, 1.0, part))

    norms = split3(norm)
    if is_left:
        parts = [with_norm(high, n) for n in norms] + [middle, middle, low]
    else:
        parts = [with_norm(p, n) for p, n in zip((high, middle, low), norms)] + [high, middle, high]
    return jnp.concatenate(parts, axis=0).astype(BF16)


def quarter_phi(squared):
    squared = jnp.maximum(squared, TINY)
    radial = squared * lax.rsqrt(squared)
    remain = jnp.maximum(1.0 - radial, 0.0)
    remain2 = remain * remain
    return (remain2 * remain2) * (radial + 0.25)


def stack_split(vector):
    high, low = split2(vector)
    return jnp.concatenate([high, low], axis=0), high


def split_product(stacked, high, weights_high, weights_low):
    both = dot(stacked, weights_high)
    rows = high.shape[0]
    return both[:rows] + both[rows:] + dot(high, weights_low)


def pack_kernel(centers, shifts, out):
    out[...] = jnp.zeros_like(out)
    out[:, 0:3, :] = jnp.broadcast_to(shifts[...][None], (out.shape[0],) + shifts.shape)
    out[:, 4:7, :] = jnp.broadcast_to(centers[...][None], (out.shape[0],) + centers.shape)


def lead_rows(value, count):
    row = lax.broadcasted_iota(jnp.int32, value.shape, value.ndim - 2)
    return jnp.where(row < count, value, 0.0)


def build_kernel(me, every, high_ref, low_ref, applied_out, left_ref):
    parts = every.shape[0]
    mine = every[me[0]]
    left_ref[...] = features(mine, True)

    def block(number, total):
        there = every[number]
        right = features(there, False)
        weights = quarter_phi(dot(right, left_ref[...], LEFT_T))
        weights_high, weights_low = split2(weights)
        high_ref[number] = weights_high
        low_ref[number] = weights_low
        stacked, high = stack_split(4.0 * lead_rows(there, 3))
        return total + split_product(stacked, high, weights_high, weights_low)

    total = lax.fori_loop(0, parts, block, jnp.zeros(mine.shape, F32))
    applied = total + SHIFT * lead_rows(mine, 3)
    applied_out[...] = jnp.broadcast_to(applied[0:4][None], applied_out.shape)


def matvec(vector_ref, high_ref, low_ref):
    parts, rows, width = vector_ref.shape

    def block(number, total):
        stacked, high = stack_split(4.0 * vector_ref[number])
        return total + split_product(stacked, high, high_ref[number], low_ref[number])

    return lax.fori_loop(0, parts, block, jnp.zeros((rows, width), F32))


def whole_sum(value):
    return jnp.sum(jnp.sum(value, axis=0), axis=1, keepdims=True)


def ratio(top, bottom):
    row = lax.broadcasted_iota(jnp.int32, top.shape, 0)
    return jnp.where(row < 3, top / jnp.where(row < 3, bottom, 1.0), 0.0)


def turn_one_kernel(me, every, applied, high_ref, low_ref, applied_out, search_out, remain_out, numbers_out):
    start = lead_rows(every[:, 0:4, :], 3)
    got = applied[...]
    norm = whole_sum(start * start)
    step = ratio(norm, whole_sum(start * got))
    remain = start - step[None] * got
    following = whole_sum(remain * remain)
    search = remain + ratio(following, norm)[None] * start
    search_out[:, 0:4, :] = search
    search_out[:, 4:8, :] = jnp.zeros_like(search)
    remain_out[...] = remain
    numbers_out[0] = jnp.broadcast_to(step, numbers_out.shape[1:])
    numbers_out[1] = jnp.broadcast_to(following, numbers_out.shape[1:])
    product = matvec(search_out, high_ref, low_ref)
    product = product[0:4] + SHIFT * search_out[me[0]][0:4]
    applied_out[...] = jnp.broadcast_to(product[None], applied_out.shape)


def turn_two_kernel(me, every, applied, search_in, remain_in, numbers, high_ref, low_ref, partial_out, pair_out, norm_out):
    start = lead_rows(every[:, 0:4, :], 3)
    got = applied[...]
    search = search_in[:, 0:4, :]
    norm = numbers[1][:, 0:1]
    step = ratio(norm, whole_sum(search * got))
    iterate = numbers[0][:, 0:1][None] * start + step[None] * search
    remain = remain_in[...] - step[None] * got
    following = whole_sum(remain * remain)
    search = remain + ratio(following, norm)[None] * search
    pair_out[:, 0:4, :] = search
    pair_out[:, 4:8, :] = iterate
    norm_out[...] = jnp.broadcast_to(following, norm_out.shape)
    product = matvec(pair_out, high_ref, low_ref)
    mine = pair_out[me[0]][0:4]
    product = product[0:4] + SHIFT * mine
    partial = jnp.sum(mine * product, axis=1, keepdims=True)
    partial_out[...] = jnp.broadcast_to(partial[None], partial_out.shape)


def edge_kernel(every, points, pair, out, left_ref):
    parts = every.shape[0]
    width = out.shape[1]
    piece = min(width, 256)
    left_ref[...] = features(points[...], True)
    out[...] = jnp.zeros_like(out)

    def block(number, carry):
        right = features(every[number], False).T
        stacked, high = stack_split(4.0 * pair[number])
        for first in range(0, width, piece):
            cols = slice(first, first + piece)
            weights = quarter_phi(dot(right, left_ref[:, cols]))
            out[:, cols] += split_product(stacked, high, *split2(weights))
        return carry

    lax.fori_loop(0, parts, block, 0)


def pick_kernel(me, send_list, partials, norm, pair, motions, coefficients_out, tiles_out, edge_ref):
    total = jnp.sum(partials[...], axis=0)[:, 0:1]
    step = ratio(norm[:, 0:1], total)
    mine = pair[me[0]]
    coefficients_out[...] = (mine[4:8] + step * mine[0:4])[0:3]
    motion = motions[4:8, :] + step * motions[0:4, :]
    for edge in range(edge_ref.shape[0]):
        edge_ref[edge] = motion[:, edge * S : (edge + 1) * S]
    for place in range(tiles_out.shape[0]):
        for position in range(tiles_out.shape[1]):
            tiles_out[place, position] = edge_ref[jnp.maximum(send_list[place, position], 0)]


def blend(index):
    fraction = index.astype(F32) / (S - 1)
    return 1.0 - fraction, fraction


def six_products(left, right):
    lh, lm, ll = split3(left)
    rh, rm, rl = split3(right)
    lefts = jnp.concatenate([lh, lh, lm, lh, ll, lm], axis=0).astype(BF16)
    rights = jnp.concatenate([rh, rm, rh, rl, rh, rm], axis=0).astype(BF16)
    return dot(lefts, rights, LEFT_T)


def block_kernel(block_tiles, count, tiles, out, tile_ref, spread_ref, weight_ref):
    slot = pl.program_id(0)
    cells = S * S

    @pl.when(slot == 0)
    def _():
        index = lax.broadcasted_iota(jnp.int32, (2 * S, cells), 0)
        cell = lax.broadcasted_iota(jnp.int32, (2 * S, cells), 1)
        wanted = jnp.where(index < S, cell // S, cell % S + S)
        spread_ref[...] = jnp.where(index == wanted, 1.0, 0.0).astype(BF16)
        row = lax.broadcasted_iota(jnp.int32, (8, cells), 0)
        cell = lax.broadcasted_iota(jnp.int32, (8, cells), 1)
        j_low, j_high = blend(cell // S)
        k_low, k_high = blend(cell % S)
        j_weight = jnp.where(row % 2 == 0, j_low, j_high)
        k_weight = jnp.where(row // 2 == 0, k_low, k_high)
        weight_ref[0] = jnp.where(row < 4, j_weight * k_weight, 0.0)
        side = row % 4 // 2 == 0
        weight_ref[1] = jnp.where(row < 4, jnp.where(side, k_low, k_high), jnp.where(side, j_low, j_high))

    @pl.when(slot < count[0])
    def _():
        for edge in range(12):
            tile = tiles[block_tiles[slot, edge]]
            for coordinate in range(3):
                tile_ref[coordinate, edge : edge + 1, :] = tile[coordinate : coordinate + 1, :]
        along_low, along_high = blend(lax.broadcasted_iota(jnp.int32, (8, S), 1))
        row = lax.broadcasted_iota(jnp.int32, (8, S), 0)
        side = jnp.where(row % 2 == 0, along_low, along_high)
        for coordinate in range(3):
            first = tile_ref[coordinate, 0:8, :]
            straight = along_low * first[:, 0:1] + along_high * first[:, S - 1 : S]
            bent = jnp.where(row < 4, first - 2.0 * straight, 0.0)
            others = tile_ref[coordinate, 4:12, :]
            zero = jnp.zeros_like(others)
            placed = jnp.concatenate(
                [jnp.where(row < 4, others, zero), jnp.where(row < 4, zero, others)], axis=1
            )
            spread = dot(jnp.concatenate(split3(placed), axis=0).astype(BF16), spread_ref[...])
            spread = (spread[0:8] + spread[8:16]) + spread[16:24]
            lefts = jnp.concatenate([bent, side], axis=0)
            rights = jnp.concatenate([weight_ref[0], spread * weight_ref[1]], axis=0)
            out[0, coordinate] = six_products(lefts, rights)

    @pl.when(slot >= count[0])
    def _():
        out[...] = jnp.zeros_like(out)


def call(kernel, name, outs, specs, scratch=(), **more):
    shapes = tuple(jax.ShapeDtypeStruct(shape, dtype) for shape, dtype in outs)
    return pl.pallas_call(
        kernel,
        out_shape=shapes,
        in_specs=specs,
        out_specs=tuple(VMEM for _ in shapes),
        scratch_shapes=scratch,
        compiler_params=pltpu.CompilerParams(vmem_limit_bytes=48 << 20),
        name=name,
        **more,
    )


def shards(total, center_points, displacements, edge_points, send_list, block_tiles, block_count):
    width = center_points.shape[1]
    edge_width = edge_points.shape[1]
    group = send_list.shape[1]
    capacity = send_list.shape[2]
    slots = block_tiles.shape[0]
    me = (lax.axis_index("gx") * lax.axis_size("gy") + lax.axis_index("gy")).reshape(1)

    def spread_out(copies, axes):
        return lax.all_to_all(copies, axes, split_axis=0, concat_axis=0, tiled=True)

    (packed,) = call(pack_kernel, "pack", [((total, 8, width), F32)], [VMEM] * 2)(center_points, displacements)
    every = spread_out(packed, BOTH)
    matrix = ((total, width, width), BF16)
    thin = ((total, 4, width), F32)
    wide = ((total, 8, width), F32)
    high, low, applied = call(
        build_kernel, "build", [matrix, matrix, thin], [SMEM, VMEM], [pltpu.VMEM((48, width), BF16)]
    )(me, every)
    applied = spread_out(applied, BOTH)
    applied, search, remain, numbers = call(
        turn_one_kernel, "turn_one", [thin, wide, thin, ((2, 4, 128), F32)], [SMEM] + [VMEM] * 4
    )(me, every, applied, high, low)
    applied = spread_out(applied, BOTH)
    partials, pair, norm = call(
        turn_two_kernel, "turn_two", [((total, 4, 128), F32), wide, ((4, 128), F32)], [SMEM] + [VMEM] * 7
    )(me, every, applied, search, remain, numbers, high, low)
    partials = spread_out(partials, BOTH)
    points = jnp.concatenate([jnp.zeros((4, edge_width), F32), edge_points, jnp.zeros((1, edge_width), F32)])
    (motions,) = call(
        edge_kernel, "edges", [((8, edge_width), F32)], [VMEM] * 3, [pltpu.VMEM((48, edge_width), BF16)]
    )(every, points, pair)
    coefficients, tiles = call(
        pick_kernel,
        "pick",
        [((3, width), F32), ((group, capacity, 4, S), F32)],
        [SMEM] * 2 + [VMEM] * 4,
        [pltpu.VMEM((edge_width // S, 4, S), F32)],
    )(me, send_list[0], partials, norm, pair, motions)
    tiles = spread_out(tiles, "gy").reshape(group * capacity, 4, S)
    block_motion = pl.pallas_call(
        block_kernel,
        out_shape=jax.ShapeDtypeStruct((slots, 3, S, S * S), F32),
        grid=(slots,),
        in_specs=[SMEM, SMEM, VMEM],
        out_specs=pl.BlockSpec((1, 3, S, S * S), lambda slot: (slot, 0, 0, 0)),
        scratch_shapes=[
            pltpu.VMEM((3, 12, S), F32),
            pltpu.VMEM((2 * S, S * S), BF16),
            pltpu.VMEM((2, 8, S * S), F32),
        ],
        compiler_params=pltpu.CompilerParams(vmem_limit_bytes=48 << 20),
        name="blocks",
    )(block_tiles, block_count, tiles)
    return coefficients, block_motion


def solution(mesh):
    total = mesh.shape["gx"] * mesh.shape["gy"]
    split = P(None, BOTH)
    return jax.shard_map(
        functools.partial(shards, total),
        mesh=mesh,
        in_specs=(split, split, split, P(BOTH, None, None), P(BOTH, None), P(BOTH)),
        out_specs=(split, P(BOTH, None, None, None)),
        check_vma=False,
    )
```

```python
import functools
import math

import jax
import jax.numpy as jnp
from jax import lax
from jax.experimental import pallas as pl
from jax.experimental.pallas import tpu as pltpu
from jax.sharding import PartitionSpec as P

S = 64
SHIFT = 0.1
INV_RADIUS = 4.0
TINY = 1e-12
BOTH = ("gx", "gy")
F32, BF16 = jnp.float32, jnp.bfloat16
VMEM = pl.BlockSpec(memory_space=pltpu.VMEM)
SMEM = pl.BlockSpec(memory_space=pltpu.SMEM)
PLAIN = (((1,), (0,)), ((), ()))
LEFT_T = (((0,), (0,)), ((), ()))


def dot(left, right, dims=PLAIN):
    return lax.dot_general(left, right, dims, preferred_element_type=F32)


def split2(value):
    high = value.astype(BF16)
    return high, (value - high.astype(F32)).astype(BF16)


def split3(value):
    high = value.astype(BF16).astype(F32)
    rest = value - high
    middle = rest.astype(BF16).astype(F32)
    return high, middle, rest - middle


def features(points, is_left):
    row = lax.broadcasted_iota(jnp.int32, points.shape, 0)
    is_point = (row >= 4) & (row < 7)
    scaled = jnp.where(is_point, (points - 0.5) * INV_RADIUS, 0.0)
    norm = jnp.sum(scaled * scaled, axis=0, keepdims=True)
    own_row, other_row = (0, 1) if is_left else (1, 0)
    if is_left:
        scaled = -2.0 * scaled
    high, middle, low = split3(scaled)

    def with_norm(part, norm_part):
        return jnp.where(row == own_row, norm_part, jnp.where(row == other_row, 1.0, part))

    norms = split3(norm)
    if is_left:
        parts = [with_norm(high, n) for n in norms] + [middle, middle, low]
    else:
        parts = [with_norm(p, n) for p, n in zip((high, middle, low), norms)] + [high, middle, high]
    return jnp.concatenate(parts, axis=0).astype(BF16)


def quarter_phi(squared):
    squared = jnp.maximum(squared, TINY)
    radial = squared * lax.rsqrt(squared)
    remain = jnp.maximum(1.0 - radial, 0.0)
    remain2 = remain * remain
    return (remain2 * remain2) * (radial + 0.25)


def stack_split(vector):
    high, low = split2(vector)
    return jnp.concatenate([high, low], axis=0), high


def split_product(stacked, high, weights_high, weights_low):
    both = dot(stacked, weights_high)
    rows = high.shape[0]
    return both[:rows] + both[rows:] + dot(high, weights_low)


def pack_kernel(centers, shifts, out):
    out[...] = jnp.zeros_like(out)
    out[:, 0:3, :] = jnp.broadcast_to(shifts[...][None], (out.shape[0],) + shifts.shape)
    out[:, 4:7, :] = jnp.broadcast_to(centers[...][None], (out.shape[0],) + centers.shape)


def lead_rows(value, count):
    row = lax.broadcasted_iota(jnp.int32, value.shape, value.ndim - 2)
    return jnp.where(row < count, value, 0.0)


def flat(ref):
    return jnp.concatenate([ref[part] for part in range(ref.shape[0])], axis=1)


def fill_weights(right_ref, left_ref, high_ref, low_ref):
    extent = right_ref.shape[0]
    step = math.gcd(extent, 1024)
    for first in range(0, extent, step):
        rows = slice(first, first + step)
        weights = quarter_phi(dot(right_ref[rows, :], left_ref[...]))
        high_ref[rows, :], low_ref[rows, :] = split2(weights)


def matvec(vector, high_ref, low_ref):
    stacked, high = stack_split(4.0 * vector)
    return split_product(stacked, high, high_ref[...], low_ref[...])


def build_kernel(me, every, right_ref, high_ref, low_ref, applied_out, left_ref):
    everything = flat(every)
    mine = every[me[0]]
    left_ref[...] = features(mine, True)
    right_ref[...] = features(everything, False).T
    fill_weights(right_ref, left_ref, high_ref, low_ref)
    applied = matvec(lead_rows(everything, 3), high_ref, low_ref) + SHIFT * lead_rows(mine, 3)
    applied_out[...] = jnp.broadcast_to(applied[0:4][None], applied_out.shape)


def edge_weights_kernel(first, after, right_ref, points, high_ref, low_ref, left_ref, padded_ref):
    padded_ref[...] = jnp.zeros_like(padded_ref)
    padded_ref[4:7, :] = points[:, first : first + left_ref.shape[1]]
    left_ref[...] = features(padded_ref[...], True)
    fill_weights(right_ref, left_ref, high_ref, low_ref)


def edge_motion_kernel(pair, high_ref, low_ref, out):
    out[...] = matvec(pair[...], high_ref, low_ref)


def lane_sum(value):
    return jnp.sum(value, axis=1, keepdims=True)


def ratio(top, bottom):
    row = lax.broadcasted_iota(jnp.int32, top.shape, 0)
    return jnp.where(row < 3, top / jnp.where(row < 3, bottom, 1.0), 0.0)


def own_part(ref, me, width):
    if width % 128 == 0:
        return ref[:, pl.ds(pl.multiple_of(me * width, 128), width)]
    lane = lax.broadcasted_iota(jnp.int32, (ref.shape[1], width), 0)
    column = lax.broadcasted_iota(jnp.int32, (ref.shape[1], width), 1)
    chosen = jnp.where(lane == me * width + column, 1.0, 0.0)
    return lax.dot_general(ref[...], chosen, PLAIN, precision=lax.Precision.HIGHEST, preferred_element_type=F32)


def turn_one_kernel(me, every, applied, high_ref, low_ref, applied_out, search_out, remain_out, numbers_out):
    width = every.shape[2]
    start = lead_rows(flat(every), 3)[0:4]
    got = flat(applied)
    norm = lane_sum(start * start)
    step = ratio(norm, lane_sum(start * got))
    remain = start - step * got
    following = lane_sum(remain * remain)
    search = remain + ratio(following, norm) * start
    search_out[...] = search
    remain_out[...] = remain
    numbers_out[0] = jnp.broadcast_to(step, numbers_out.shape[1:])
    numbers_out[1] = jnp.broadcast_to(following, numbers_out.shape[1:])
    product = matvec(jnp.concatenate([search, jnp.zeros_like(search)], axis=0), high_ref, low_ref)
    product = product[0:4] + SHIFT * own_part(search_out, me[0], width)
    applied_out[...] = jnp.broadcast_to(product[None], applied_out.shape)


def turn_two_kernel(me, every, applied, search_in, remain_in, numbers, high_ref, low_ref, partial_out, pair_out, norm_out):
    width = every.shape[2]
    start = lead_rows(flat(every), 3)[0:4]
    got = flat(applied)
    search = search_in[...]
    norm = numbers[1][:, 0:1]
    step = ratio(norm, lane_sum(search * got))
    iterate = numbers[0][:, 0:1] * start + step * search
    remain = remain_in[...] - step * got
    following = lane_sum(remain * remain)
    search = remain + ratio(following, norm) * search
    pair = jnp.concatenate([search, iterate], axis=0)
    pair_out[...] = pair
    norm_out[...] = jnp.broadcast_to(following, norm_out.shape)
    product = matvec(pair, high_ref, low_ref)
    mine = own_part(pair_out, me[0], width)[0:4]
    product = product[0:4] + SHIFT * mine
    partial_out[...] = jnp.broadcast_to(lane_sum(mine * product)[None], partial_out.shape)


def pick_kernel(me, send_list, partials, norm, pair, *rest):
    motions, (coefficients_out, tiles_out, edge_ref) = rest[:-3], rest[-3:]
    total = jnp.sum(partials[...], axis=0)[:, 0:1]
    step = ratio(norm[:, 0:1], total)
    mine = own_part(pair, me[0], coefficients_out.shape[1])
    coefficients_out[...] = (mine[4:8] + step * mine[0:4])[0:3]
    edge = 0
    for part in motions:
        motion = part[4:8, :] + step * part[0:4, :]
        for first in range(0, motion.shape[1], S):
            edge_ref[edge] = motion[:, first : first + S]
            edge += 1
    group, capacity = tiles_out.shape[0], tiles_out.shape[1] // 4
    for place in range(group):
        for position in range(capacity):
            tile = edge_ref[jnp.maximum(send_list[place, position], 0)]
            tiles_out[place, 4 * position : 4 * position + 4, 0:S] = tile


def blend(index):
    fraction = index.astype(F32) / (S - 1)
    return 1.0 - fraction, fraction


def six_products(left, right):
    lh, lm, ll = split3(left)
    rh, rm, rl = split3(right)
    lefts = jnp.concatenate([lh, lh, lm, lh, ll, lm], axis=0).astype(BF16)
    rights = jnp.concatenate([rh, rm, rh, rl, rh, rm], axis=0).astype(BF16)
    return dot(lefts, rights, LEFT_T)


def block_kernel(block_tiles, count, tiles, out, tile_ref, spread_ref, weight_ref):
    slot = pl.program_id(0)
    cells = S * S
    capacity = tiles.shape[1] // 4

    @pl.when(slot == 0)
    def _():
        index = lax.broadcasted_iota(jnp.int32, (2 * S, cells), 0)
        cell = lax.broadcasted_iota(jnp.int32, (2 * S, cells), 1)
        wanted = jnp.where(index < S, cell // S, cell % S + S)
        spread_ref[...] = jnp.where(index == wanted, 1.0, 0.0).astype(BF16)
        row = lax.broadcasted_iota(jnp.int32, (8, cells), 0)
        cell = lax.broadcasted_iota(jnp.int32, (8, cells), 1)
        j_low, j_high = blend(cell // S)
        k_low, k_high = blend(cell % S)
        j_weight = jnp.where(row % 2 == 0, j_low, j_high)
        k_weight = jnp.where(row // 2 == 0, k_low, k_high)
        weight_ref[0] = jnp.where(row < 4, j_weight * k_weight, 0.0)
        side = row % 4 // 2 == 0
        weight_ref[1] = jnp.where(row < 4, jnp.where(side, k_low, k_high), jnp.where(side, j_low, j_high))

    @pl.when(slot < count[0])
    def _():
        for edge in range(12):
            place = block_tiles[slot, edge]
            tile = tiles[place // capacity, pl.ds(place % capacity * 4, 4), :]
            for coordinate in range(3):
                tile_ref[coordinate, edge : edge + 1, :] = tile[coordinate : coordinate + 1, 0:S]
        along_low, along_high = blend(lax.broadcasted_iota(jnp.int32, (8, S), 1))
        row = lax.broadcasted_iota(jnp.int32, (8, S), 0)
        side = jnp.where(row % 2 == 0, along_low, along_high)
        for coordinate in range(3):
            first = tile_ref[coordinate, 0:8, :]
            straight = along_low * first[:, 0:1] + along_high * first[:, S - 1 : S]
            bent = jnp.where(row < 4, first - 2.0 * straight, 0.0)
            others = tile_ref[coordinate, 4:12, :]
            zero = jnp.zeros_like(others)
            placed = jnp.concatenate(
                [jnp.where(row < 4, others, zero), jnp.where(row < 4, zero, others)], axis=1
            )
            spread = dot(jnp.concatenate(split3(placed), axis=0).astype(BF16), spread_ref[...])
            spread = (spread[0:8] + spread[8:16]) + spread[16:24]
            lefts = jnp.concatenate([bent, side], axis=0)
            rights = jnp.concatenate([weight_ref[0], spread * weight_ref[1]], axis=0)
            out[0, coordinate] = six_products(lefts, rights)

    @pl.when(slot >= count[0])
    def _():
        out[...] = jnp.zeros_like(out)


def call(kernel, name, outs, specs, scratch=(), megabytes=13, work=0):
    shapes = tuple(jax.ShapeDtypeStruct(shape, dtype) for shape, dtype in outs)
    return pl.pallas_call(
        kernel,
        out_shape=shapes,
        in_specs=specs,
        out_specs=tuple(VMEM for _ in shapes),
        scratch_shapes=scratch,
        compiler_params=pltpu.CompilerParams(vmem_limit_bytes=megabytes << 20),
        cost_estimate=pl.CostEstimate(flops=work, bytes_accessed=0, transcendentals=0) if work else None,
        name=name,
    )


def shards(total, center_points, displacements, edge_points, send_list, block_tiles, block_count):
    width = center_points.shape[1]
    extent = total * width
    edge_width = edge_points.shape[1]
    group, capacity = send_list.shape[1:]
    slots = block_tiles.shape[0]
    me = (lax.axis_index("gx") * lax.axis_size("gy") + lax.axis_index("gy")).reshape(1)

    def spread_out(copies, axes):
        return lax.all_to_all(copies, axes, split_axis=0, concat_axis=0, tiled=True)

    (packed,) = call(pack_kernel, "pack", [((total, 8, width), F32)], [VMEM] * 2)(center_points, displacements)
    every = spread_out(packed, BOTH)
    matrix = ((extent, width), BF16)
    thin = ((total, 4, width), F32)
    right, high, low, applied = call(
        build_kernel,
        "build",
        [((extent, 48), BF16), matrix, matrix, thin],
        [SMEM, VMEM],
        [pltpu.VMEM((48, width), BF16)],
        15,
    )(me, every)
    piece = math.gcd(edge_width, 256)
    pieces = edge_width // piece

    def edge_weights(number, after):
        part = ((extent, piece), BF16)
        return call(
            functools.partial(edge_weights_kernel, number * piece),
            "edge_weights",
            [part, part],
            [pl.BlockSpec(memory_space=pl.ANY), VMEM, VMEM],
            [pltpu.VMEM((48, piece), BF16), pltpu.VMEM((8, piece), F32)],
            13,
            extent * piece * 2000,
        )(after, right, edge_points)

    applied_all = spread_out(applied, BOTH)
    weights = [edge_weights(number, me) for number in range(pieces // 2)]
    applied, search, remain, numbers = call(
        turn_one_kernel,
        "turn_one",
        [thin, ((4, extent), F32), ((4, extent), F32), ((2, 4, 128), F32)],
        [SMEM] + [VMEM] * 4,
    )(me, every, applied_all, high, low)
    applied_all = spread_out(applied, BOTH)
    weights += [edge_weights(number, numbers) for number in range(pieces // 2, pieces)]
    partials, pair, norm = call(
        turn_two_kernel,
        "turn_two",
        [((total, 4, 128), F32), ((8, extent), F32), ((4, 128), F32)],
        [SMEM] + [VMEM] * 7,
    )(me, every, applied_all, search, remain, numbers, high, low)
    partials = spread_out(partials, BOTH)
    motions = [
        call(edge_motion_kernel, "edge_motion", [((8, piece), F32)], [VMEM] * 3, (), 13, extent * piece * 1000)(
            pair, *pieces_of
        )[0]
        for pieces_of in weights
    ]
    coefficients, tiles = call(
        pick_kernel,
        "pick",
        [((3, width), F32), ((group, capacity * 4, 128), F32)],
        [SMEM] * 2 + [VMEM] * (3 + pieces),
        [pltpu.VMEM((edge_width // S, 4, S), F32)],
    )(me, send_list[0], partials, norm, pair, *motions)
    tiles = spread_out(tiles, "gy")
    block_motion = pl.pallas_call(
        block_kernel,
        out_shape=jax.ShapeDtypeStruct((slots, 3, S, S * S), F32),
        grid=(slots,),
        in_specs=[SMEM, SMEM, VMEM],
        out_specs=pl.BlockSpec((1, 3, S, S * S), lambda slot: (slot, 0, 0, 0)),
        scratch_shapes=[
            pltpu.VMEM((3, 12, S), F32),
            pltpu.VMEM((2 * S, S * S), BF16),
            pltpu.VMEM((2, 8, S * S), F32),
        ],
        compiler_params=pltpu.CompilerParams(vmem_limit_bytes=24 << 20),
        name="blocks",
    )(block_tiles, block_count, tiles)
    return coefficients, block_motion


def solution(mesh):
    total = mesh.shape["gx"] * mesh.shape["gy"]
    split = P(None, BOTH)
    return jax.shard_map(
        functools.partial(shards, total),
        mesh=mesh,
        in_specs=(split, split, split, P(BOTH, None, None), P(BOTH, None), P(BOTH)),
        out_specs=(split, P(BOTH, None, None, None)),
        check_vma=False,
    )
```

```python
import functools
import math

import jax
import jax.numpy as jnp
from jax import lax
from jax.experimental import pallas as pl
from jax.experimental.pallas import tpu as pltpu
from jax.sharding import PartitionSpec as P

S = 64
SHIFTS = S.bit_length() - 1
SHIFT = 0.1
INV_RADIUS = 4.0
TINY = 1e-12
BOTH = ("gx", "gy")
LARGE = 56
F32, BF16 = jnp.float32, jnp.bfloat16
ANY = pl.BlockSpec(memory_space=pl.ANY)
VMEM = pl.BlockSpec(memory_space=pltpu.VMEM)
SMEM = pl.BlockSpec(memory_space=pltpu.SMEM)
PLAIN = (((1,), (0,)), ((), ()))
LEFT_T = (((0,), (0,)), ((), ()))


def dot(left, right, dims=PLAIN):
    return lax.dot_general(left, right, dims, preferred_element_type=F32)


def split2(value):
    high = value.astype(BF16)
    return high, (value - high.astype(F32)).astype(BF16)


def split3(value):
    high = value.astype(BF16).astype(F32)
    rest = value - high
    middle = rest.astype(BF16).astype(F32)
    return high, middle, rest - middle


def features(points, is_left):
    row = lax.broadcasted_iota(jnp.int32, points.shape, 0)
    is_point = (row >= 4) & (row < 7)
    scaled = jnp.where(is_point, (points - 0.5) * INV_RADIUS, 0.0)
    norm = jnp.sum(scaled * scaled, axis=0, keepdims=True)
    own_row, other_row = (0, 1) if is_left else (1, 0)
    if is_left:
        scaled = -2.0 * scaled
    high, middle, low = split3(scaled)

    def with_norm(part, norm_part):
        return jnp.where(row == own_row, norm_part, jnp.where(row == other_row, 1.0, part))

    norms = split3(norm)
    if is_left:
        parts = [with_norm(high, n) for n in norms] + [middle, middle, low]
    else:
        parts = [with_norm(p, n) for p, n in zip((high, middle, low), norms)] + [high, middle, high]
    return jnp.concatenate(parts, axis=0).astype(BF16)


def quarter_phi(squared):
    squared = jnp.maximum(squared, TINY)
    remain = jnp.maximum(1.0 - squared * lax.rsqrt(squared), 0.0)
    remain2 = remain * remain
    return (remain2 * remain2) * (1.25 - remain)


def pack_kernel(centers, shifts, out, centers_ref, shifts_ref, done):
    copies = [
        pltpu.make_async_copy(centers, centers_ref, done.at[0]),
        pltpu.make_async_copy(shifts, shifts_ref, done.at[1]),
    ]
    for copy in copies:
        copy.start()
    out[...] = jnp.zeros_like(out)
    for copy in copies:
        copy.wait()
    out[:, 0:3, :] = jnp.broadcast_to(shifts_ref[...][None], (out.shape[0],) + shifts.shape)
    out[:, 4:7, :] = jnp.broadcast_to(centers_ref[...][None], (out.shape[0],) + centers.shape)


def lead_rows(value, count):
    row = lax.broadcasted_iota(jnp.int32, value.shape, value.ndim - 2)
    return jnp.where(row < count, value, 0.0)


def flat(ref):
    return jnp.concatenate([ref[part] for part in range(ref.shape[0])], axis=1)


def whole_slice(number, size):
    return pl.ds(pl.multiple_of(number * size, size), size)


def keep_vector(vector, kept_ref):
    both = jnp.concatenate(split2(4.0 * vector), axis=0)
    points = kept_ref.shape[2]
    for number in range(kept_ref.shape[0]):
        kept_ref[number] = both[:, number * points : (number + 1) * points]


def end_sum(both):
    rows = both.shape[0] // 2
    return both[:rows] + both[rows:]


def made_product(right_ref, left_ref, kept_ref, inside, store=None):
    pieces, rows, size = kept_ref.shape
    width = left_ref.shape[1]
    step_columns = math.gcd(width, 256)
    columns = [slice(first, first + step_columns) for first in range(0, width, step_columns)]
    inside = math.gcd(pieces, inside)

    def one_round(turn, sums):
        sums = list(sums)
        for step in range(inside):
            number = turn * inside + step
            for place, piece in enumerate(columns):
                squared = dot(right_ref[whole_slice(number, size), :], left_ref[:, piece])
                weights = split2(quarter_phi(squared))
                if store is not None:
                    for held, part in zip(store, weights):
                        held[whole_slice(number, size), piece] = part
                for part in weights:
                    sums[place] += dot(kept_ref[number], part)
        return tuple(sums)

    start = tuple(jnp.zeros((rows, step_columns), F32) for _ in columns)
    sums = lax.fori_loop(0, pieces // inside, one_round, start)
    return [(piece, end_sum(both)) for piece, both in zip(columns, sums)]


def kept_product(vector, high_ref, low_ref):
    both = jnp.concatenate(split2(4.0 * vector), axis=0)
    return end_sum(dot(both, high_ref[...]) + dot(both, low_ref[...]))


def build_kernel(me, every, right_ref, high_ref, low_ref, applied_out, left_ref, kept_ref):
    everything = flat(every)
    mine = every[me[0]]
    left_ref[...] = features(mine, True)
    right_ref[...] = features(everything, False).T
    keep_vector(lead_rows(everything, 3), kept_ref)
    ((_, product),) = made_product(right_ref, left_ref, kept_ref, 8, (high_ref, low_ref))
    applied = product + SHIFT * lead_rows(mine, 3)
    applied_out[...] = jnp.broadcast_to(applied[0:4][None], applied_out.shape)


def edge_kernel(right_ref, points, pair, out, left_ref, padded_ref, kept_ref):
    padded_ref[...] = jnp.zeros_like(padded_ref)
    padded_ref[4:7, :] = points[...]
    left_ref[...] = features(padded_ref[...], True)
    keep_vector(pair[...], kept_ref)
    for piece, product in made_product(right_ref, left_ref, kept_ref, 4):
        out[:, piece] = product


def lane_sum(value):
    return jnp.sum(value, axis=1, keepdims=True)


def ratio(top, bottom):
    row = lax.broadcasted_iota(jnp.int32, top.shape, 0)
    return jnp.where(row < 3, top / jnp.where(row < 3, bottom, 1.0), 0.0)


def own_part(ref, me, width):
    if width % 128 == 0:
        return ref[:, pl.ds(pl.multiple_of(me * width, 128), width)]
    lane = lax.broadcasted_iota(jnp.int32, (ref.shape[1], width), 0)
    column = lax.broadcasted_iota(jnp.int32, (ref.shape[1], width), 1)
    chosen = jnp.where(lane == me * width + column, 1.0, 0.0)
    return lax.dot_general(ref[...], chosen, PLAIN, precision=lax.Precision.HIGHEST, preferred_element_type=F32)


def turn_one_kernel(me, every, applied, high_ref, low_ref, applied_out, search_out, remain_out, numbers_out):
    width = every.shape[2]
    start = lead_rows(flat(every), 3)[0:4]
    got = flat(applied)
    norm = lane_sum(start * start)
    step = ratio(norm, lane_sum(start * got))
    remain = start - step * got
    following = lane_sum(remain * remain)
    search = remain + ratio(following, norm) * start
    search_out[...] = search
    remain_out[...] = remain
    numbers_out[0] = jnp.broadcast_to(step, numbers_out.shape[1:])
    numbers_out[1] = jnp.broadcast_to(following, numbers_out.shape[1:])
    product = kept_product(jnp.concatenate([search, jnp.zeros_like(search)], axis=0), high_ref, low_ref)
    product = product[0:4] + SHIFT * own_part(search_out, me[0], width)
    applied_out[...] = jnp.broadcast_to(product[None], applied_out.shape)


def turn_two_kernel(me, every, applied, search_in, remain_in, numbers, high_ref, low_ref, partial_out, pair_out, norm_out):
    width = every.shape[2]
    start = lead_rows(flat(every), 3)[0:4]
    got = flat(applied)
    search = search_in[...]
    norm = numbers[1][:, 0:1]
    step = ratio(norm, lane_sum(search * got))
    iterate = numbers[0][:, 0:1] * start + step * search
    remain = remain_in[...] - step * got
    following = lane_sum(remain * remain)
    search = remain + ratio(following, norm) * search
    pair = jnp.concatenate([search, iterate], axis=0)
    pair_out[...] = pair
    norm_out[...] = jnp.broadcast_to(following, norm_out.shape)
    product = kept_product(pair, high_ref, low_ref)
    mine = own_part(pair_out, me[0], width)[0:4]
    product = product[0:4] + SHIFT * mine
    partial_out[...] = jnp.broadcast_to(lane_sum(mine * product)[None], partial_out.shape)


def last_step(partials, norm):
    return ratio(norm[:, 0:1], jnp.sum(partials[...], axis=0)[:, 0:1])


def coefficients_kernel(me, partials, norm, pair, out):
    mine = own_part(pair, me[0], out.shape[1])
    out[...] = (mine[4:8] + last_step(partials, norm) * mine[0:4])[0:3]


def pick_kernel(send_list, partials, norm, motions, tiles_out, edge_ref):
    motion = motions[4:8, :] + last_step(partials, norm) * motions[0:4, :]
    for edge in range(edge_ref.shape[0]):
        edge_ref[edge] = motion[:, edge * S : (edge + 1) * S]
    group, capacity = send_list.shape
    for place in range(group):
        for position in range(0, capacity, 2):
            here = [
                edge_ref[jnp.maximum(send_list[place, number], 0)]
                for number in (position, min(position + 1, capacity - 1))
            ]
            tiles_out[place, 2 * position : 2 * position + 4, :] = jnp.concatenate(here, axis=1)


def blend(index):
    fraction = index.astype(F32) / (S - 1)
    return 1.0 - fraction, fraction


def six_products(left, right):
    lh, lm, ll = split3(left)
    rh, rm, rl = split3(right)
    lefts = jnp.concatenate([lh, lh, lm, lh, ll, lm], axis=0).astype(BF16)
    rights = jnp.concatenate([rh, rm, rh, rl, rh, rm], axis=0).astype(BF16)
    return dot(lefts, rights, LEFT_T)


def block_kernel(block_tiles, count, tiles, out, tile_ref, spread_ref, weight_ref):
    slot, coordinate = pl.program_id(0), pl.program_id(1)
    cells = S * S
    capacity = block_tiles.shape[0] * block_tiles.shape[1] // tiles.shape[0]

    @pl.when((slot == 0) & (coordinate == 0))
    def _():
        index = lax.broadcasted_iota(jnp.int32, (S, 2 * S), 0)
        lane = lax.broadcasted_iota(jnp.int32, (S, 2 * S), 1)
        half = jnp.where(lane < S, 0, 1)
        third = jnp.where(index == lane - S * half, 1.0, 0.0).astype(BF16)
        for first in range(0, cells, 2 * S):
            columns = slice(first, first + 2 * S)
            spread_ref[0:S, columns] = jnp.where(index - first // S == half, 1.0, 0.0).astype(BF16)
            spread_ref[S : 2 * S, columns] = third
        row = lax.broadcasted_iota(jnp.int32, (8, cells), 0)
        cell = lax.broadcasted_iota(jnp.int32, (8, cells), 1)
        j_low, j_high = blend(cell >> SHIFTS)
        k_low, k_high = blend(cell & (S - 1))
        j_weight = jnp.where(row & 1 == 0, j_low, j_high)
        k_weight = jnp.where(row < 2, k_low, k_high)
        weight_ref[0] = jnp.where(row < 4, j_weight * k_weight, 0.0)
        side = row & 2 == 0
        weight_ref[1] = jnp.where(row < 4, jnp.where(side, k_low, k_high), jnp.where(side, j_low, j_high))

    @pl.when((slot < count[0]) & (coordinate == 0))
    def _():
        for edge in range(12):
            place = block_tiles[slot, edge]
            source = lax.div(place, capacity)
            position = place - source * capacity
            group = lax.div(position, 2)
            pair = tiles[source, pl.ds(4 * group, 4), :]
            tile = jnp.where(position == 2 * group, pair[:, 0:S], pair[:, S : 2 * S])
            for row in range(3):
                tile_ref[row, edge : edge + 1, :] = tile[row : row + 1, :]

    @pl.when(slot < count[0])
    def _():
        along_low, along_high = blend(lax.broadcasted_iota(jnp.int32, (8, S), 1))
        row = lax.broadcasted_iota(jnp.int32, (8, S), 0)
        side = jnp.where(row & 1 == 0, along_low, along_high)
        first = tile_ref[coordinate, 0:8, :]
        straight = along_low * first[:, 0:1] + along_high * first[:, S - 1 : S]
        bent = jnp.where(row < 4, first - 2.0 * straight, 0.0)
        others = tile_ref[coordinate, 4:12, :]
        zero = jnp.zeros_like(others)
        placed = jnp.concatenate([jnp.where(row < 4, others, zero), jnp.where(row < 4, zero, others)], axis=1)
        spread = dot(jnp.concatenate(split3(placed), axis=0).astype(BF16), spread_ref[...])
        spread = (spread[0:8] + spread[8:16]) + spread[16:24]
        lefts = jnp.concatenate([bent, side], axis=0)
        rights = jnp.concatenate([weight_ref[0], spread * weight_ref[1]], axis=0)
        out[0, 0] = six_products(lefts, rights)

    @pl.when(slot >= count[0])
    def _():
        out[...] = jnp.zeros_like(out)


def call(kernel, name, outs, specs, scratch=(), megabytes=13, **more):
    shapes = tuple(jax.ShapeDtypeStruct(shape, dtype) for shape, dtype in outs)
    return pl.pallas_call(
        kernel,
        out_shape=shapes,
        in_specs=specs,
        scratch_shapes=scratch,
        compiler_params=pltpu.CompilerParams(vmem_limit_bytes=megabytes << 20),
        cost_estimate=pl.CostEstimate(flops=1, bytes_accessed=1, transcendentals=0),
        name=name,
        **{"out_specs": tuple(VMEM for _ in shapes), **more},
    )


def shards(total, center_points, displacements, edge_points, send_list, block_tiles, block_count):
    width = center_points.shape[1]
    extent = total * width
    edge_width = edge_points.shape[1]
    group, capacity = send_list.shape[1:]
    slots = block_tiles.shape[0]
    me = (lax.axis_index("gx") * lax.axis_size("gy") + lax.axis_index("gy")).reshape(1)

    def spread_out(copies, axes):
        return lax.all_to_all(copies, axes, split_axis=0, concat_axis=0, tiled=True)

    (packed,) = call(
        pack_kernel,
        "pack",
        [((total, 8, width), F32)],
        [ANY] * 2,
        [pltpu.VMEM((3, width), F32)] * 2 + [pltpu.SemaphoreType.DMA((2,))],
        LARGE,
    )(center_points, displacements)
    every = spread_out(packed, BOTH)
    matrix = ((extent, width), BF16)
    thin = ((total, 4, width), F32)
    size = math.gcd(extent, 512)
    kept = pltpu.VMEM((extent // size, 16, size), BF16)
    right, high, low, applied = call(
        build_kernel,
        "build",
        [((extent, 48), BF16), matrix, matrix, thin],
        [SMEM, VMEM],
        [pltpu.VMEM((48, width), BF16), kept],
    )(me, every)
    applied = spread_out(applied, BOTH)
    applied, search, remain, numbers = call(
        turn_one_kernel,
        "turn_one",
        [thin, ((4, extent), F32), ((4, extent), F32), ((2, 4, 128), F32)],
        [SMEM] + [VMEM] * 4,
    )(me, every, applied, high, low)
    applied = spread_out(applied, BOTH)
    partials, pair, norm = call(
        turn_two_kernel,
        "turn_two",
        [((total, 4, 128), F32), ((8, extent), F32), ((4, 128), F32)],
        [SMEM] + [VMEM] * 7,
    )(me, every, applied, search, remain, numbers, high, low)
    partials = spread_out(partials, BOTH)
    (motions,) = call(
        edge_kernel,
        "edges",
        [((8, edge_width), F32)],
        [VMEM] * 3,
        [pltpu.VMEM((48, edge_width), BF16), pltpu.VMEM((8, edge_width), F32), kept],
    )(right, edge_points, pair)
    (tiles,) = call(
        pick_kernel,
        "pick",
        [((group, (capacity + 1) // 2 * 4, 128), F32)],
        [SMEM] + [VMEM] * 3,
        [pltpu.VMEM((edge_width // S, 4, S), F32)],
    )(send_list[0], partials, norm, motions)
    tiles = spread_out(tiles, "gy")
    (coefficients,) = call(coefficients_kernel, "coefficients", [((3, width), F32)], [SMEM] + [VMEM] * 3)(
        me, partials, norm, pair
    )
    (block_motion,) = call(
        block_kernel,
        "blocks",
        [((slots, 3, S, S * S), F32)],
        [SMEM, SMEM, VMEM],
        [
            pltpu.VMEM((3, 12, S), F32),
            pltpu.VMEM((2 * S, S * S), BF16),
            pltpu.VMEM((2, 8, S * S), F32),
        ],
        grid=(slots, 3),
        out_specs=(pl.BlockSpec((1, 1, S, S * S), lambda slot, coordinate: (slot, coordinate, 0, 0)),),
    )(block_tiles, block_count, tiles)
    return coefficients, block_motion


def solution(mesh):
    total = mesh.shape["gx"] * mesh.shape["gy"]
    split = P(None, BOTH)
    return jax.shard_map(
        functools.partial(shards, total),
        mesh=mesh,
        in_specs=(split, split, split, P(BOTH, None, None), P(BOTH, None), P(BOTH)),
        out_specs=(split, P(BOTH, None, None, None)),
        check_vma=False,
    )
```

```python
import functools
import math

import jax
import jax.numpy as jnp
from jax import lax
from jax.experimental import pallas as pl
from jax.experimental.pallas import tpu as pltpu
from jax.sharding import PartitionSpec as P

S = 64
SHIFTS = S.bit_length() - 1
SHIFT = 0.1
INV_RADIUS = 4.0
TINY = 1e-12
BOTH = ("gx", "gy")
LARGE = 56
F32, BF16 = jnp.float32, jnp.bfloat16
ANY = pl.BlockSpec(memory_space=pl.ANY)
VMEM = pl.BlockSpec(memory_space=pltpu.VMEM)
SMEM = pl.BlockSpec(memory_space=pltpu.SMEM)
PLAIN = (((1,), (0,)), ((), ()))
LEFT_T = (((0,), (0,)), ((), ()))


def dot(left, right, dims=PLAIN):
    return lax.dot_general(left, right, dims, preferred_element_type=F32)


def split2(value):
    high = value.astype(BF16)
    return high, (value - high.astype(F32)).astype(BF16)


def split3(value):
    high = value.astype(BF16).astype(F32)
    rest = value - high
    middle = rest.astype(BF16).astype(F32)
    return high, middle, rest - middle


def features(points, is_left):
    row = lax.broadcasted_iota(jnp.int32, points.shape, 0)
    is_point = (row >= 4) & (row < 7)
    scaled = jnp.where(is_point, (points - 0.5) * INV_RADIUS, 0.0)
    norm = jnp.sum(scaled * scaled, axis=0, keepdims=True)
    own_row, other_row = (0, 1) if is_left else (1, 0)
    if is_left:
        scaled = -2.0 * scaled
    high, middle, low = split3(scaled)

    def with_norm(part, norm_part):
        return jnp.where(row == own_row, norm_part, jnp.where(row == other_row, 1.0, part))

    norms = split3(norm)
    if is_left:
        parts = [with_norm(high, n) for n in norms] + [middle, middle, low]
    else:
        parts = [with_norm(p, n) for p, n in zip((high, middle, low), norms)] + [high, middle, high]
    return jnp.concatenate(parts, axis=0).astype(BF16)


def quarter_phi(squared):
    squared = jnp.maximum(squared, TINY)
    remain = jnp.maximum(1.0 - squared * lax.rsqrt(squared), 0.0)
    remain2 = remain * remain
    return (remain2 * remain2) * (1.25 - remain)


def write_copies(rows, out, first=0):
    width = rows.shape[1]
    for number in range(3):
        place = (first + number) * width
        out[:, :, place : place + width] = jnp.broadcast_to(rows[number : number + 1][None], (out.shape[0], 1, width))


def read_copies(ref, width, first=0):
    rows = []
    for number in range(3):
        place = (first + number) * width
        rows.append(jnp.concatenate([ref[part, :, place : place + width] for part in range(ref.shape[0])], axis=1))
    return jnp.concatenate(rows + [jnp.zeros_like(rows[0])], axis=0)


def pack_kernel(centers, shifts, out, centers_ref, shifts_ref, done):
    copies = [
        pltpu.make_async_copy(centers, centers_ref, done.at[0]),
        pltpu.make_async_copy(shifts, shifts_ref, done.at[1]),
    ]
    for copy in copies:
        copy.start()
    for copy in copies:
        copy.wait()
    write_copies(shifts_ref[...], out)
    write_copies(centers_ref[...], out, 3)


def whole_slice(number, size):
    return pl.ds(pl.multiple_of(number * size, size), size)


def keep_vector(vector, kept_ref):
    both = jnp.concatenate(split2(4.0 * vector), axis=0)
    points = kept_ref.shape[2]
    for number in range(kept_ref.shape[0]):
        kept_ref[number] = both[:, number * points : (number + 1) * points]


def end_sum(both):
    rows = both.shape[0] // 2
    return both[:rows] + both[rows:]


def made_product(right_ref, left_ref, kept_ref, inside, store=None):
    pieces, rows, size = kept_ref.shape
    width = left_ref.shape[1]
    step_columns = math.gcd(width, 256)
    columns = [slice(first, first + step_columns) for first in range(0, width, step_columns)]
    inside = math.gcd(pieces, inside)

    def one_round(turn, sums):
        sums = list(sums)
        for step in range(inside):
            number = turn * inside + step
            for place, piece in enumerate(columns):
                squared = dot(right_ref[whole_slice(number, size), :], left_ref[:, piece])
                weights = split2(quarter_phi(squared))
                if store is not None:
                    for held, part in zip(store, weights):
                        held[whole_slice(number, size), piece] = part
                for part in weights:
                    sums[place] += dot(kept_ref[number], part)
        return tuple(sums)

    start = tuple(jnp.zeros((rows, step_columns), F32) for _ in columns)
    sums = lax.fori_loop(0, pieces // inside, one_round, start)
    return [(piece, end_sum(both)) for piece, both in zip(columns, sums)]


def kept_product(vector, high_ref, low_ref):
    both = jnp.concatenate(split2(4.0 * vector), axis=0)
    return end_sum(dot(both, high_ref[...]) + dot(both, low_ref[...]))


def build_kernel(me, packed, every_out, right_ref, high_ref, low_ref, applied_out, left_ref, kept_ref):
    width = left_ref.shape[1]
    shifts = read_copies(packed, width)
    centers = read_copies(packed, width, 3)
    every_out[0:4, :] = shifts
    every_out[4:8, :] = centers
    mine = own_part(every_out, me[0], width)
    left_ref[...] = features(mine, True)
    right_ref[...] = features(every_out[...], False).T
    keep_vector(jnp.concatenate([shifts, jnp.zeros_like(shifts)], axis=0), kept_ref)
    ((_, product),) = made_product(right_ref, left_ref, kept_ref, 8, (high_ref, low_ref))
    write_copies(product[0:4] + SHIFT * mine[0:4], applied_out)


def edge_kernel(right_ref, points, pair, out, left_ref, padded_ref, kept_ref):
    padded_ref[...] = jnp.zeros_like(padded_ref)
    padded_ref[4:7, :] = points[...]
    left_ref[...] = features(padded_ref[...], True)
    keep_vector(pair[...], kept_ref)
    for piece, product in made_product(right_ref, left_ref, kept_ref, 4):
        out[:, piece] = product


def lane_sum(value):
    return jnp.sum(value, axis=1, keepdims=True)


def ratio(top, bottom):
    row = lax.broadcasted_iota(jnp.int32, top.shape, 0)
    return jnp.where(row < 3, top / jnp.where(row < 3, bottom, 1.0), 0.0)


def own_part(ref, me, width):
    if width % 128 == 0:
        return ref[:, pl.ds(pl.multiple_of(me * width, 128), width)]
    lane = lax.broadcasted_iota(jnp.int32, (ref.shape[1], width), 0)
    column = lax.broadcasted_iota(jnp.int32, (ref.shape[1], width), 1)
    chosen = jnp.where(lane == me * width + column, 1.0, 0.0)
    return lax.dot_general(ref[...], chosen, PLAIN, precision=lax.Precision.HIGHEST, preferred_element_type=F32)


def turn_one_kernel(me, every, applied, high_ref, low_ref, applied_out, search_out, remain_out, numbers_out):
    width = high_ref.shape[1]
    start = every[0:4, :]
    got = read_copies(applied, width)
    norm = lane_sum(start * start)
    step = ratio(norm, lane_sum(start * got))
    remain = start - step * got
    following = lane_sum(remain * remain)
    search = remain + ratio(following, norm) * start
    search_out[...] = search
    remain_out[...] = remain
    numbers_out[0] = jnp.broadcast_to(step, numbers_out.shape[1:])
    numbers_out[1] = jnp.broadcast_to(following, numbers_out.shape[1:])
    product = kept_product(jnp.concatenate([search, jnp.zeros_like(search)], axis=0), high_ref, low_ref)
    write_copies(product[0:4] + SHIFT * own_part(search_out, me[0], width), applied_out)


def turn_two_kernel(me, every, applied, search_in, remain_in, numbers, high_ref, low_ref, partial_out, pair_out, norm_out):
    width = high_ref.shape[1]
    start = every[0:4, :]
    got = read_copies(applied, width)
    search = search_in[...]
    norm = numbers[1][:, 0:1]
    step = ratio(norm, lane_sum(search * got))
    iterate = numbers[0][:, 0:1] * start + step * search
    remain = remain_in[...] - step * got
    following = lane_sum(remain * remain)
    search = remain + ratio(following, norm) * search
    pair = jnp.concatenate([search, iterate], axis=0)
    pair_out[...] = pair
    norm_out[...] = jnp.broadcast_to(following, norm_out.shape)
    product = kept_product(pair, high_ref, low_ref)
    mine = own_part(pair_out, me[0], width)[0:4]
    product = product[0:4] + SHIFT * mine
    partial_out[...] = jnp.broadcast_to(lane_sum(mine * product)[None], partial_out.shape)


def last_step(partials, norm):
    return ratio(norm[:, 0:1], jnp.sum(partials[...], axis=0)[:, 0:1])


def coefficients_kernel(me, partials, norm, pair, out):
    mine = own_part(pair, me[0], out.shape[1])
    out[...] = (mine[4:8] + last_step(partials, norm) * mine[0:4])[0:3]


def pick_kernel(send_list, partials, norm, motions, tiles_out, edge_ref):
    motion = motions[4:8, :] + last_step(partials, norm) * motions[0:4, :]
    for edge in range(edge_ref.shape[0]):
        edge_ref[edge] = motion[:, edge * S : (edge + 1) * S]
    group, capacity = send_list.shape
    for place in range(group):
        for position in range(0, capacity, 2):
            here = [
                edge_ref[jnp.maximum(send_list[place, number], 0)]
                for number in (position, min(position + 1, capacity - 1))
            ]
            tiles_out[place, 2 * position : 2 * position + 4, :] = jnp.concatenate(here, axis=1)


def blend(index):
    fraction = index.astype(F32) / (S - 1)
    return 1.0 - fraction, fraction


def three_products(left, right):
    left_high, left_low = split2(left)
    right_high, right_low = split2(right)
    lefts = jnp.concatenate([left_high, left_high, left_low], axis=0)
    rights = jnp.concatenate([right_high, right_low, right_high], axis=0)
    return dot(lefts, rights, LEFT_T)


def block_kernel(block_tiles, count, tiles, out, tile_ref, spread_ref, weight_ref, held_ref, done):
    slots = out.shape[0]
    cells = S * S
    capacity = block_tiles.shape[0] * block_tiles.shape[1] // tiles.shape[0]
    halves = done.shape[2]

    def copies(slot, coordinate):
        rows = S // halves
        return [
            pltpu.make_async_copy(
                held_ref.at[slot, coordinate, pl.ds(half * rows, rows), :],
                out.at[slot, coordinate, pl.ds(half * rows, rows), :],
                done.at[slot, coordinate, half],
            )
            for half in range(halves)
        ]

    index = lax.broadcasted_iota(jnp.int32, (S, 2 * S), 0)
    lane = lax.broadcasted_iota(jnp.int32, (S, 2 * S), 1)
    half = jnp.where(lane < S, 0, 1)
    third = jnp.where(index == lane - S * half, 1.0, 0.0).astype(BF16)
    for first in range(0, cells, 2 * S):
        columns = slice(first, first + 2 * S)
        spread_ref[0:S, columns] = jnp.where(index - first // S == half, 1.0, 0.0).astype(BF16)
        spread_ref[S : 2 * S, columns] = third
    row = lax.broadcasted_iota(jnp.int32, (8, cells), 0)
    cell = lax.broadcasted_iota(jnp.int32, (8, cells), 1)
    j_low, j_high = blend(cell >> SHIFTS)
    k_low, k_high = blend(cell & (S - 1))
    j_weight = jnp.where(row & 1 == 0, j_low, j_high)
    k_weight = jnp.where(row < 2, k_low, k_high)
    weight_ref[0] = jnp.where(row < 4, j_weight * k_weight, 0.0)
    lower = row & 2 == 0
    weight_ref[1] = jnp.where(row < 4, jnp.where(lower, k_low, k_high), jnp.where(lower, j_low, j_high))

    along_low, along_high = blend(lax.broadcasted_iota(jnp.int32, (8, S), 1))
    row = lax.broadcasted_iota(jnp.int32, (8, S), 0)
    side = jnp.where(row & 1 == 0, along_low, along_high)

    def fill(slot, carry):
        for edge in range(12):
            place = block_tiles[slot, edge]
            source = lax.div(place, capacity)
            position = place - source * capacity
            group = lax.div(position, 2)
            pair = tiles[source, pl.ds(4 * group, 4), :]
            tile = jnp.where(position == 2 * group, pair[:, 0:S], pair[:, S : 2 * S])
            for coordinate in range(3):
                tile_ref[coordinate, edge : edge + 1, :] = tile[coordinate : coordinate + 1, :]
        for coordinate in range(3):
            first = tile_ref[coordinate, 0:8, :]
            straight = along_low * first[:, 0:1] + along_high * first[:, S - 1 : S]
            bent = jnp.where(row < 4, first - 2.0 * straight, 0.0)
            others = tile_ref[coordinate, 4:12, :]
            zero = jnp.zeros_like(others)
            placed = jnp.concatenate([jnp.where(row < 4, others, zero), jnp.where(row < 4, zero, others)], axis=1)
            spread = end_sum(dot(jnp.concatenate(split2(placed), axis=0), spread_ref[...]))
            lefts = jnp.concatenate([bent, side], axis=0)
            rights = jnp.concatenate([weight_ref[0], spread * weight_ref[1]], axis=0)
            held_ref[slot, coordinate] = three_products(lefts, rights)
            for copy in copies(slot, coordinate):
                copy.start()
        return carry

    def clear(slot, carry):
        held_ref[slot] = jnp.zeros_like(held_ref[slot])
        for coordinate in range(3):
            for copy in copies(slot, coordinate):
                copy.start()
        return carry

    lax.fori_loop(0, count[0], fill, 0)
    lax.fori_loop(count[0], slots, clear, 0)
    for slot in range(slots):
        for coordinate in range(3):
            for copy in copies(slot, coordinate):
                copy.wait()


def call(kernel, name, outs, specs, scratch=(), megabytes=13, **more):
    shapes = tuple(jax.ShapeDtypeStruct(shape, dtype) for shape, dtype in outs)
    return pl.pallas_call(
        kernel,
        out_shape=shapes,
        in_specs=specs,
        scratch_shapes=scratch,
        compiler_params=pltpu.CompilerParams(vmem_limit_bytes=megabytes << 20),
        cost_estimate=pl.CostEstimate(flops=1, bytes_accessed=1, transcendentals=0),
        name=name,
        **{"out_specs": tuple(VMEM for _ in shapes), **more},
    )


def shards(total, center_points, displacements, edge_points, send_list, block_tiles, block_count):
    width = center_points.shape[1]
    extent = total * width
    edge_width = edge_points.shape[1]
    group, capacity = send_list.shape[1:]
    slots = block_tiles.shape[0]
    me = (lax.axis_index("gx") * lax.axis_size("gy") + lax.axis_index("gy")).reshape(1)

    def spread_out(copies, axes):
        return lax.all_to_all(copies, axes, split_axis=0, concat_axis=0, tiled=True)

    (packed,) = call(
        pack_kernel,
        "pack",
        [((total, 1, 6 * width), F32)],
        [ANY] * 2,
        [pltpu.VMEM((3, width), F32)] * 2 + [pltpu.SemaphoreType.DMA((2,))],
        LARGE,
    )(center_points, displacements)
    packed = spread_out(packed, BOTH)
    matrix = ((extent, width), BF16)
    thin = ((total, 1, 3 * width), F32)
    size = math.gcd(extent, 512)
    kept = pltpu.VMEM((extent // size, 16, size), BF16)
    every, right, high, low, applied = call(
        build_kernel,
        "build",
        [((8, extent), F32), ((extent, 48), BF16), matrix, matrix, thin],
        [SMEM, VMEM],
        [pltpu.VMEM((48, width), BF16), kept],
    )(me, packed)
    applied = spread_out(applied, BOTH)
    applied, search, remain, numbers = call(
        turn_one_kernel,
        "turn_one",
        [thin, ((4, extent), F32), ((4, extent), F32), ((2, 4, 128), F32)],
        [SMEM] + [VMEM] * 4,
    )(me, every, applied, high, low)
    applied = spread_out(applied, BOTH)
    partials, pair, norm = call(
        turn_two_kernel,
        "turn_two",
        [((total, 4, 128), F32), ((8, extent), F32), ((4, 128), F32)],
        [SMEM] + [VMEM] * 7,
    )(me, every, applied, search, remain, numbers, high, low)
    partials = spread_out(partials, BOTH)
    (motions,) = call(
        edge_kernel,
        "edges",
        [((8, edge_width), F32)],
        [VMEM] * 3,
        [pltpu.VMEM((48, edge_width), BF16), pltpu.VMEM((8, edge_width), F32), kept],
    )(right, edge_points, pair)
    (tiles,) = call(
        pick_kernel,
        "pick",
        [((group, (capacity + 1) // 2 * 4, 128), F32)],
        [SMEM] + [VMEM] * 3,
        [pltpu.VMEM((edge_width // S, 4, S), F32)],
    )(send_list[0], partials, norm, motions)
    tiles = spread_out(tiles, "gy")
    (coefficients,) = call(coefficients_kernel, "coefficients", [((3, width), F32)], [SMEM] + [VMEM] * 3)(
        me, partials, norm, pair
    )
    (block_motion,) = call(
        block_kernel,
        "blocks",
        [((slots, 3, S, S * S), F32)],
        [SMEM, SMEM, VMEM],
        [
            pltpu.VMEM((3, 12, S), F32),
            pltpu.VMEM((2 * S, S * S), BF16),
            pltpu.VMEM((2, 8, S * S), F32),
            pltpu.VMEM((slots, 3, S, S * S), F32),
            pltpu.SemaphoreType.DMA((slots, 3, 2)),
        ],
        24,
        out_specs=(ANY,),
    )(block_tiles, block_count, tiles)
    return coefficients, block_motion


def solution(mesh):
    total = mesh.shape["gx"] * mesh.shape["gy"]
    split = P(None, BOTH)
    return jax.shard_map(
        functools.partial(shards, total),
        mesh=mesh,
        in_specs=(split, split, split, P(BOTH, None, None), P(BOTH, None), P(BOTH)),
        out_specs=(split, P(BOTH, None, None, None)),
        check_vma=False,
    )
```

```python
import functools
import math

import jax
import jax.numpy as jnp
from jax import lax
from jax.experimental import pallas as pl
from jax.experimental.pallas import tpu as pltpu
from jax.sharding import PartitionSpec as P

S = 64
SHIFTS = S.bit_length() - 1
SHIFT = 0.1
INV_RADIUS = 4.0
TINY = 1e-12
BOTH = ("gx", "gy")
LARGE = 56
F32, BF16 = jnp.float32, jnp.bfloat16
ANY = pl.BlockSpec(memory_space=pl.ANY)
VMEM = pl.BlockSpec(memory_space=pltpu.VMEM)
SMEM = pl.BlockSpec(memory_space=pltpu.SMEM)
PLAIN = (((1,), (0,)), ((), ()))
LEFT_T = (((0,), (0,)), ((), ()))


def dot(left, right, dims=PLAIN):
    return lax.dot_general(left, right, dims, preferred_element_type=F32)


def split2(value):
    high = value.astype(BF16)
    return high, (value - high.astype(F32)).astype(BF16)


def split3(value):
    high = value.astype(BF16).astype(F32)
    rest = value - high
    middle = rest.astype(BF16).astype(F32)
    return high, middle, rest - middle


def features(points, is_left):
    row = lax.broadcasted_iota(jnp.int32, points.shape, 0)
    is_point = (row >= 4) & (row < 7)
    scaled = jnp.where(is_point, (points - 0.5) * INV_RADIUS, 0.0)
    norm = jnp.sum(scaled * scaled, axis=0, keepdims=True)
    own_row, other_row = (0, 1) if is_left else (1, 0)
    if is_left:
        scaled = -2.0 * scaled
    high, middle, low = split3(scaled)

    def with_norm(part, norm_part):
        return jnp.where(row == own_row, norm_part, jnp.where(row == other_row, 1.0, part))

    norms = split3(norm)
    if is_left:
        parts = [with_norm(high, n) for n in norms] + [middle, middle, low]
    else:
        parts = [with_norm(p, n) for p, n in zip((high, middle, low), norms)] + [high, middle, high]
    return jnp.concatenate(parts, axis=0).astype(BF16)


def quarter_phi(squared):
    squared = jnp.maximum(squared, TINY)
    radial = pltpu.reciprocal(lax.rsqrt(squared), approx=True)
    remain = jnp.maximum(1.0 - radial, 0.0)
    remain2 = remain * remain
    return (remain2 * remain2) * (1.25 - remain)


def write_copies(rows, out, first=0):
    width = rows.shape[1]
    for number in range(3):
        place = (first + number) * width
        out[:, :, place : place + width] = jnp.broadcast_to(rows[number : number + 1][None], (out.shape[0], 1, width))


def read_copies(ref, width, first=0):
    rows = []
    for number in range(3):
        place = (first + number) * width
        rows.append(jnp.concatenate([ref[part, :, place : place + width] for part in range(ref.shape[0])], axis=1))
    return jnp.concatenate(rows + [jnp.zeros_like(rows[0])], axis=0)


def pack_kernel(centers, shifts, out, centers_ref, shifts_ref, done):
    copies = [
        pltpu.make_async_copy(centers, centers_ref, done.at[0]),
        pltpu.make_async_copy(shifts, shifts_ref, done.at[1]),
    ]
    for copy in copies:
        copy.start()
    for copy in copies:
        copy.wait()
    write_copies(shifts_ref[...], out)
    write_copies(centers_ref[...], out, 3)


def whole_slice(number, size):
    return pl.ds(pl.multiple_of(number * size, size), size)


def keep_vector(vector, kept_ref):
    both = jnp.concatenate(split2(4.0 * vector), axis=0)
    points = kept_ref.shape[2]
    for number in range(kept_ref.shape[0]):
        kept_ref[number] = both[:, number * points : (number + 1) * points]


def end_sum(both):
    rows = both.shape[0] // 2
    return both[:rows] + both[rows:]


def made_product(right_ref, left_ref, kept_ref, inside, store=None):
    pieces, rows, size = kept_ref.shape
    width = left_ref.shape[1]
    step_columns = math.gcd(width, 256)
    columns = [slice(first, first + step_columns) for first in range(0, width, step_columns)]
    inside = math.gcd(pieces, inside)

    def one_round(turn, sums):
        sums = list(sums)
        for step in range(inside):
            number = turn * inside + step
            for place, piece in enumerate(columns):
                squared = dot(right_ref[whole_slice(number, size), :], left_ref[:, piece])
                weights = split2(quarter_phi(squared))
                if store is not None:
                    for held, part in zip(store, weights):
                        held[whole_slice(number, size), piece] = part
                for part in weights:
                    sums[place] += dot(kept_ref[number], part)
        return tuple(sums)

    start = tuple(jnp.zeros((rows, step_columns), F32) for _ in columns)
    sums = lax.fori_loop(0, pieces // inside, one_round, start)
    return [(piece, end_sum(both)) for piece, both in zip(columns, sums)]


def kept_product(vector, high_ref, low_ref):
    both = jnp.concatenate(split2(4.0 * vector), axis=0)
    return end_sum(dot(both, high_ref[...]) + dot(both, low_ref[...]))


def build_kernel(me, packed, tables, wanted, every_out, right_ref, high_ref, low_ref, applied_out, left_ref, kept_ref):
    width = left_ref.shape[1]
    shifts = read_copies(packed, width)
    centers = read_copies(packed, width, 3)
    every_out[0:4, :] = shifts
    every_out[4:8, :] = centers
    mine = own_part(every_out, me[0], width)
    left_ref[...] = features(mine, True)
    right_ref[...] = features(every_out[...], False).T
    keep_vector(jnp.concatenate([shifts, jnp.zeros_like(shifts)], axis=0), kept_ref)
    ((_, product),) = made_product(right_ref, left_ref, kept_ref, 8, (high_ref, low_ref))
    write_copies(product[0:4] + SHIFT * mine[0:4], applied_out)


def edge_kernel(right_ref, points, pair, out, left_ref, padded_ref, kept_ref):
    padded_ref[...] = jnp.zeros_like(padded_ref)
    padded_ref[4:7, :] = points[...]
    left_ref[...] = features(padded_ref[...], True)
    keep_vector(pair[...], kept_ref)
    for piece, product in made_product(right_ref, left_ref, kept_ref, 4):
        out[:, piece] = product


def lane_sum(value):
    return jnp.sum(value, axis=1, keepdims=True)


def ratio(top, bottom):
    row = lax.broadcasted_iota(jnp.int32, top.shape, 0)
    return jnp.where(row < 3, top / jnp.where(row < 3, bottom, 1.0), 0.0)


def own_part(ref, me, width):
    if width % 128 == 0:
        return ref[:, pl.ds(pl.multiple_of(me * width, 128), width)]
    lane = lax.broadcasted_iota(jnp.int32, (ref.shape[1], width), 0)
    column = lax.broadcasted_iota(jnp.int32, (ref.shape[1], width), 1)
    chosen = jnp.where(lane == me * width + column, 1.0, 0.0)
    return lax.dot_general(ref[...], chosen, PLAIN, precision=lax.Precision.HIGHEST, preferred_element_type=F32)


def turn_one_kernel(me, every, applied, high_ref, low_ref, applied_out, search_out, remain_out, numbers_out):
    width = high_ref.shape[1]
    start = every[0:4, :]
    got = read_copies(applied, width)
    norm = lane_sum(start * start)
    step = ratio(norm, lane_sum(start * got))
    remain = start - step * got
    following = lane_sum(remain * remain)
    search = remain + ratio(following, norm) * start
    search_out[...] = search
    remain_out[...] = remain
    numbers_out[0] = jnp.broadcast_to(step, numbers_out.shape[1:])
    numbers_out[1] = jnp.broadcast_to(following, numbers_out.shape[1:])
    product = kept_product(jnp.concatenate([search, jnp.zeros_like(search)], axis=0), high_ref, low_ref)
    write_copies(product[0:4] + SHIFT * own_part(search_out, me[0], width), applied_out)


def turn_two_kernel(me, every, applied, search_in, remain_in, numbers, high_ref, low_ref, partial_out, pair_out, norm_out):
    width = high_ref.shape[1]
    start = every[0:4, :]
    got = read_copies(applied, width)
    search = search_in[...]
    norm = numbers[1][:, 0:1]
    step = ratio(norm, lane_sum(search * got))
    iterate = numbers[0][:, 0:1] * start + step * search
    remain = remain_in[...] - step * got
    following = lane_sum(remain * remain)
    search = remain + ratio(following, norm) * search
    pair = jnp.concatenate([search, iterate], axis=0)
    pair_out[...] = pair
    norm_out[...] = jnp.broadcast_to(following, norm_out.shape)
    product = kept_product(pair, high_ref, low_ref)
    mine = own_part(pair_out, me[0], width)[0:4]
    product = product[0:4] + SHIFT * mine
    partial = lane_sum(mine * product)
    lane = lax.broadcasted_iota(jnp.int32, (1, partial_out.shape[2]), 1)
    row = jnp.zeros(lane.shape, F32)
    for number in range(3):
        row = jnp.where(lane == number, partial[number : number + 1], row)
    partial_out[...] = jnp.broadcast_to(row[None], partial_out.shape)


def last_step(partials, norm):
    row = jnp.sum(partials[...], axis=0)
    number = lax.broadcasted_iota(jnp.int32, (4, 1), 0)
    total = jnp.ones((4, 1), F32)
    for coordinate in range(3):
        total = jnp.where(number == coordinate, row[:, coordinate : coordinate + 1], total)
    return ratio(norm[:, 0:1], total)


def pick_kernel(send_list, partials, norm, motions, tiles_out, edge_ref):
    motion = motions[4:8, :] + last_step(partials, norm) * motions[0:4, :]
    for edge in range(edge_ref.shape[0]):
        edge_ref[edge] = motion[:, edge * S : (edge + 1) * S]
    group, capacity = send_list.shape
    for place in range(group):
        for position in range(0, capacity, 2):
            here = [
                edge_ref[jnp.maximum(send_list[place, number], 0)]
                for number in (position, min(position + 1, capacity - 1))
            ]
            tiles_out[place, 2 * position : 2 * position + 4, :] = jnp.concatenate(here, axis=1)


def blend(index):
    fraction = index.astype(F32) / (S - 1)
    return 1.0 - fraction, fraction


def three_products(left, right):
    left_high, left_low = split2(left)
    right_high, right_low = split2(right)
    lefts = jnp.concatenate([left_high, left_high, left_low], axis=0)
    rights = jnp.concatenate([right_high, right_low, right_high], axis=0)
    return dot(lefts, rights, LEFT_T)


def block_kernel(me, tables, tiles, partials, norm, pair, out, coefficients_out, *scratch):
    tile_ref, spread_ref, weight_ref, held_ref, coefficients_ref, done, coefficients_done = scratch
    slots = out.shape[0]
    cells = S * S
    capacity = slots * 12 // tiles.shape[0]
    live = tables[0, 12]
    halves = done.shape[2]

    def copies(slot, coordinate):
        rows = S // halves
        return [
            pltpu.make_async_copy(
                held_ref.at[slot, coordinate, pl.ds(half * rows, rows), :],
                out.at[slot, coordinate, pl.ds(half * rows, rows), :],
                done.at[slot, coordinate, half],
            )
            for half in range(halves)
        ]

    index = lax.broadcasted_iota(jnp.int32, (S, 2 * S), 0)
    lane = lax.broadcasted_iota(jnp.int32, (S, 2 * S), 1)
    half = jnp.where(lane < S, 0, 1)
    third = jnp.where(index == lane - S * half, 1.0, 0.0).astype(BF16)
    for first in range(0, cells, 2 * S):
        columns = slice(first, first + 2 * S)
        spread_ref[0:S, columns] = jnp.where(index - first // S == half, 1.0, 0.0).astype(BF16)
        spread_ref[S : 2 * S, columns] = third
    row = lax.broadcasted_iota(jnp.int32, (8, cells), 0)
    cell = lax.broadcasted_iota(jnp.int32, (8, cells), 1)
    j_low, j_high = blend(cell >> SHIFTS)
    k_low, k_high = blend(cell & (S - 1))
    j_weight = jnp.where(row & 1 == 0, j_low, j_high)
    k_weight = jnp.where(row < 2, k_low, k_high)
    weight_ref[0] = jnp.where(row < 4, j_weight * k_weight, 0.0)
    lower = row & 2 == 0
    weight_ref[1] = jnp.where(row < 4, jnp.where(lower, k_low, k_high), jnp.where(lower, j_low, j_high))

    along_low, along_high = blend(lax.broadcasted_iota(jnp.int32, (8, S), 1))
    row = lax.broadcasted_iota(jnp.int32, (8, S), 0)
    side = jnp.where(row & 1 == 0, along_low, along_high)

    def fill(slot, carry):
        for edge in range(12):
            place = tables[slot, edge]
            source = lax.div(place, capacity)
            position = place - source * capacity
            group = lax.div(position, 2)
            pair = tiles[source, pl.ds(4 * group, 4), :]
            tile = jnp.where(position == 2 * group, pair[:, 0:S], pair[:, S : 2 * S])
            for coordinate in range(3):
                tile_ref[coordinate, edge : edge + 1, :] = tile[coordinate : coordinate + 1, :]
        for coordinate in range(3):
            first = tile_ref[coordinate, 0:8, :]
            straight = along_low * first[:, 0:1] + along_high * first[:, S - 1 : S]
            bent = jnp.where(row < 4, first - 2.0 * straight, 0.0)
            others = tile_ref[coordinate, 4:12, :]
            zero = jnp.zeros_like(others)
            placed = jnp.concatenate([jnp.where(row < 4, others, zero), jnp.where(row < 4, zero, others)], axis=1)
            spread = end_sum(dot(jnp.concatenate(split2(placed), axis=0), spread_ref[...]))
            lefts = jnp.concatenate([bent, side], axis=0)
            rights = jnp.concatenate([weight_ref[0], spread * weight_ref[1]], axis=0)
            held_ref[slot, coordinate] = three_products(lefts, rights)
            for copy in copies(slot, coordinate):
                copy.start()
        return carry

    def clear(slot, carry):
        held_ref[slot] = jnp.zeros_like(held_ref[slot])
        for coordinate in range(3):
            for copy in copies(slot, coordinate):
                copy.start()
        return carry

    lax.fori_loop(0, live, fill, 0)
    lax.fori_loop(live, slots, clear, 0)
    mine = own_part(pair, me[0], coefficients_out.shape[1])
    coefficients_ref[...] = (mine[4:8] + last_step(partials, norm) * mine[0:4])[0:3]
    last_copy = pltpu.make_async_copy(coefficients_ref, coefficients_out, coefficients_done)
    last_copy.start()
    for slot in range(slots):
        for coordinate in range(3):
            for copy in copies(slot, coordinate):
                copy.wait()
    last_copy.wait()


def call(kernel, name, outs, specs, scratch=(), megabytes=13, **more):
    shapes = tuple(jax.ShapeDtypeStruct(shape, dtype) for shape, dtype in outs)
    return pl.pallas_call(
        kernel,
        out_shape=shapes,
        in_specs=specs,
        scratch_shapes=scratch,
        compiler_params=pltpu.CompilerParams(vmem_limit_bytes=megabytes << 20),
        cost_estimate=pl.CostEstimate(flops=1, bytes_accessed=1, transcendentals=0),
        name=name,
        **{"out_specs": tuple(VMEM for _ in shapes), **more},
    )


def shards(total, center_points, displacements, edge_points, send_list, block_tiles, block_count):
    width = center_points.shape[1]
    extent = total * width
    edge_width = edge_points.shape[1]
    group, capacity = send_list.shape[1:]
    slots = block_tiles.shape[0]
    me = (lax.axis_index("gx") * lax.axis_size("gy") + lax.axis_index("gy")).reshape(1)

    wanted = send_list[0]
    tables = jnp.concatenate([block_tiles, jnp.broadcast_to(block_count[:, None], (slots, 1))], axis=1)

    def spread_out(copies, axes):
        return lax.all_to_all(copies, axes, split_axis=0, concat_axis=0, tiled=True)

    (packed,) = call(
        pack_kernel,
        "pack",
        [((total, 1, 6 * width), F32)],
        [ANY] * 2,
        [pltpu.VMEM((3, width), F32)] * 2 + [pltpu.SemaphoreType.DMA((2,))],
        LARGE,
    )(center_points, displacements)
    packed = spread_out(packed, BOTH)
    matrix = ((extent, width), BF16)
    thin = ((total, 1, 3 * width), F32)
    size = math.gcd(extent, 512)
    kept = pltpu.VMEM((extent // size, 16, size), BF16)
    every, right, high, low, applied = call(
        build_kernel,
        "build",
        [((8, extent), F32), ((extent, 48), BF16), matrix, matrix, thin],
        [SMEM, VMEM, ANY, ANY],
        [pltpu.VMEM((48, width), BF16), kept],
    )(me, packed, tables, wanted)
    applied = spread_out(applied, BOTH)
    applied, search, remain, numbers = call(
        turn_one_kernel,
        "turn_one",
        [thin, ((4, extent), F32), ((4, extent), F32), ((2, 4, 128), F32)],
        [SMEM] + [VMEM] * 4,
    )(me, every, applied, high, low)
    applied = spread_out(applied, BOTH)
    partials, pair, norm = call(
        turn_two_kernel,
        "turn_two",
        [((total, 1, 128), F32), ((8, extent), F32), ((4, 128), F32)],
        [SMEM] + [VMEM] * 7,
    )(me, every, applied, search, remain, numbers, high, low)
    partials = spread_out(partials, BOTH)
    (motions,) = call(
        edge_kernel,
        "edges",
        [((8, edge_width), F32)],
        [VMEM] * 3,
        [pltpu.VMEM((48, edge_width), BF16), pltpu.VMEM((8, edge_width), F32), kept],
    )(right, edge_points, pair)
    (tiles,) = call(
        pick_kernel,
        "pick",
        [((group, (capacity + 1) // 2 * 4, 128), F32)],
        [SMEM] + [VMEM] * 3,
        [pltpu.VMEM((edge_width // S, 4, S), F32)],
    )(wanted, partials, norm, motions)
    tiles = spread_out(tiles, "gy")
    block_motion, coefficients = call(
        block_kernel,
        "blocks",
        [((slots, 3, S, S * S), F32), ((3, width), F32)],
        [SMEM] * 2 + [VMEM] * 4,
        [
            pltpu.VMEM((3, 12, S), F32),
            pltpu.VMEM((2 * S, S * S), BF16),
            pltpu.VMEM((2, 8, S * S), F32),
            pltpu.VMEM((slots, 3, S, S * S), F32),
            pltpu.VMEM((3, width), F32),
            pltpu.SemaphoreType.DMA((slots, 3, 2)),
            pltpu.SemaphoreType.DMA,
        ],
        24,
        out_specs=(ANY, ANY),
    )(me, tables, tiles, partials, norm, pair)
    return coefficients, block_motion


def solution(mesh):
    total = mesh.shape["gx"] * mesh.shape["gy"]
    split = P(None, BOTH)
    return jax.shard_map(
        functools.partial(shards, total),
        mesh=mesh,
        in_specs=(split, split, split, P(BOTH, None, None), P(BOTH, None), P(BOTH)),
        out_specs=(split, P(BOTH, None, None, None)),
        check_vma=False,
    )
```

```python
import functools
import math

import jax
import jax.numpy as jnp
from jax import lax
from jax.experimental import pallas as pl
from jax.experimental.pallas import tpu as pltpu
from jax.sharding import PartitionSpec as P

S = 64
SHIFTS = S.bit_length() - 1
SHIFT = 0.1
INV_RADIUS = 4.0
TINY = 1e-12
BOTH = ("gx", "gy")
F32, BF16 = jnp.float32, jnp.bfloat16
ANY = pl.BlockSpec(memory_space=pl.ANY)
VMEM = pl.BlockSpec(memory_space=pltpu.VMEM)
PLAIN = (((1,), (0,)), ((), ()))
LEFT_T = (((0,), (0,)), ((), ()))


def dot(left, right, dims=PLAIN):
    return lax.dot_general(left, right, dims, preferred_element_type=F32)


def split2(value):
    high = value.astype(BF16)
    return high, (value - high.astype(F32)).astype(BF16)


def split3(value):
    high = value.astype(BF16).astype(F32)
    rest = value - high
    middle = rest.astype(BF16).astype(F32)
    return high, middle, rest - middle


def features(points, is_left):
    row = lax.broadcasted_iota(jnp.int32, points.shape, 0)
    is_point = (row >= 4) & (row < 7)
    scaled = jnp.where(is_point, (points - 0.5) * INV_RADIUS, 0.0)
    norm = jnp.sum(scaled * scaled, axis=0, keepdims=True)
    own_row, other_row = (0, 1) if is_left else (1, 0)
    if is_left:
        scaled = -2.0 * scaled
    high, middle, low = split3(scaled)

    def with_norm(part, norm_part):
        return jnp.where(row == own_row, norm_part, jnp.where(row == other_row, 1.0, part))

    norms = split3(norm)
    if is_left:
        parts = [with_norm(high, n) for n in norms] + [middle, middle, low]
    else:
        parts = [with_norm(p, n) for p, n in zip((high, middle, low), norms)] + [high, middle, high]
    return jnp.concatenate(parts, axis=0).astype(BF16)


def quarter_phi(squared):
    squared = jnp.maximum(squared, TINY)
    radial = pltpu.reciprocal(lax.rsqrt(squared), approx=True)
    remain = jnp.maximum(1.0 - radial, 0.0)
    remain2 = remain * remain
    return (remain2 * remain2) * (1.25 - remain)


def write_copies(rows, out, first=0):
    width = rows.shape[1]
    for number in range(3):
        place = (first + number) * width
        out[:, :, place : place + width] = jnp.broadcast_to(rows[number : number + 1][None], (out.shape[0], 1, width))


def read_copies(ref, width, first=0):
    rows = []
    for number in range(3):
        place = (first + number) * width
        rows.append(jnp.concatenate([ref[part, :, place : place + width] for part in range(ref.shape[0])], axis=1))
    return jnp.concatenate(rows + [jnp.zeros_like(rows[0])], axis=0)


def pack_kernel(stacked, out):
    write_copies(stacked[0:3, :], out)
    write_copies(stacked[3:6, :], out, 3)


def own_index():
    return lax.axis_index("gx") * lax.axis_size("gy") + lax.axis_index("gy")


def whole_slice(number, size):
    return pl.ds(pl.multiple_of(number * size, size), size)


def keep_vector(vector, kept_ref):
    both = jnp.concatenate(split2(4.0 * vector), axis=0)
    points = kept_ref.shape[2]
    for number in range(kept_ref.shape[0]):
        kept_ref[number] = both[:, number * points : (number + 1) * points]


def end_sum(both):
    rows = both.shape[0] // 2
    return both[:rows] + both[rows:]


def made_product(right_ref, left_ref, kept_ref, inside, store=None):
    pieces, rows, size = kept_ref.shape
    width = left_ref.shape[1]
    step_columns = math.gcd(width, 256)
    columns = [slice(first, first + step_columns) for first in range(0, width, step_columns)]
    inside = math.gcd(pieces, inside)

    def one_round(turn, sums):
        sums = list(sums)
        for step in range(inside):
            number = turn * inside + step
            for place, piece in enumerate(columns):
                squared = dot(right_ref[whole_slice(number, size), :], left_ref[:, piece])
                weights = split2(quarter_phi(squared))
                if store is not None:
                    for held, part in zip(store, weights):
                        held[whole_slice(number, size), piece] = part
                for part in weights:
                    sums[place] += dot(kept_ref[number], part)
        return tuple(sums)

    start = tuple(jnp.zeros((rows, step_columns), F32) for _ in columns)
    sums = lax.fori_loop(0, pieces // inside, one_round, start)
    return [(piece, end_sum(both)) for piece, both in zip(columns, sums)]


def kept_product(vector, high_ref, low_ref):
    both = jnp.concatenate(split2(4.0 * vector), axis=0)
    return end_sum(dot(both, high_ref[...]) + dot(both, low_ref[...]))


def build_kernel(packed, chosen, placed, every_out, right_ref, high_ref, low_ref, applied_out, left_ref, kept_ref):
    width = left_ref.shape[1]
    shifts = read_copies(packed, width)
    centers = read_copies(packed, width, 3)
    every_out[0:4, :] = shifts
    every_out[4:8, :] = centers
    mine = own_part(every_out, own_index(), width)
    left_ref[...] = features(mine, True)
    right_ref[...] = features(every_out[...], False).T
    keep_vector(jnp.concatenate([shifts, jnp.zeros_like(shifts)], axis=0), kept_ref)
    ((_, product),) = made_product(right_ref, left_ref, kept_ref, 8, (high_ref, low_ref))
    write_copies(product[0:4] + SHIFT * mine[0:4], applied_out)


def edge_kernel(right_ref, points, pair, out, left_ref, padded_ref, kept_ref):
    padded_ref[...] = jnp.zeros_like(padded_ref)
    padded_ref[4:7, :] = points[...]
    left_ref[...] = features(padded_ref[...], True)
    keep_vector(pair[...], kept_ref)
    for piece, product in made_product(right_ref, left_ref, kept_ref, 4):
        out[:, piece] = product


def lane_sum(value):
    return jnp.sum(value, axis=1, keepdims=True)


def ratio(top, bottom):
    row = lax.broadcasted_iota(jnp.int32, top.shape, 0)
    return jnp.where(row < 3, top / jnp.where(row < 3, bottom, 1.0), 0.0)


def own_part(ref, me, width):
    if width % 128 == 0:
        return ref[:, pl.ds(pl.multiple_of(me * width, 128), width)]
    lane = lax.broadcasted_iota(jnp.int32, (ref.shape[1], width), 0)
    column = lax.broadcasted_iota(jnp.int32, (ref.shape[1], width), 1)
    chosen = jnp.where(lane == me * width + column, 1.0, 0.0)
    return lax.dot_general(ref[...], chosen, PLAIN, precision=lax.Precision.HIGHEST, preferred_element_type=F32)


def turn_one_kernel(every, applied, high_ref, low_ref, applied_out, search_out, remain_out, numbers_out):
    width = high_ref.shape[1]
    start = every[0:4, :]
    got = read_copies(applied, width)
    norm = lane_sum(start * start)
    step = ratio(norm, lane_sum(start * got))
    remain = start - step * got
    following = lane_sum(remain * remain)
    search = remain + ratio(following, norm) * start
    search_out[...] = search
    remain_out[...] = remain
    numbers_out[0] = jnp.broadcast_to(step, numbers_out.shape[1:])
    numbers_out[1] = jnp.broadcast_to(following, numbers_out.shape[1:])
    product = kept_product(jnp.concatenate([search, jnp.zeros_like(search)], axis=0), high_ref, low_ref)
    write_copies(product[0:4] + SHIFT * own_part(search_out, own_index(), width), applied_out)


def turn_two_kernel(every, applied, search_in, remain_in, numbers, high_ref, low_ref, partial_out, pair_out, norm_out):
    width = high_ref.shape[1]
    start = every[0:4, :]
    got = read_copies(applied, width)
    search = search_in[...]
    norm = numbers[1][:, 0:1]
    step = ratio(norm, lane_sum(search * got))
    iterate = numbers[0][:, 0:1] * start + step * search
    remain = remain_in[...] - step * got
    following = lane_sum(remain * remain)
    search = remain + ratio(following, norm) * search
    pair = jnp.concatenate([search, iterate], axis=0)
    pair_out[...] = pair
    norm_out[...] = jnp.broadcast_to(following, norm_out.shape)
    product = kept_product(pair, high_ref, low_ref)
    mine = own_part(pair_out, own_index(), width)[0:4]
    product = product[0:4] + SHIFT * mine
    partial = lane_sum(mine * product)
    lane = lax.broadcasted_iota(jnp.int32, (1, partial_out.shape[2]), 1)
    row = jnp.zeros(lane.shape, F32)
    for number in range(3):
        row = jnp.where(lane == number, partial[number : number + 1], row)
    partial_out[...] = jnp.broadcast_to(row[None], partial_out.shape)


def last_step(partials, norm):
    row = jnp.sum(partials[...], axis=0)
    number = lax.broadcasted_iota(jnp.int32, (4, 1), 0)
    total = jnp.ones((4, 1), F32)
    for coordinate in range(3):
        total = jnp.where(number == coordinate, row[:, coordinate : coordinate + 1], total)
    return ratio(norm[:, 0:1], total)


def choose(one_hot, values):
    width = values.shape[1]
    parts = dot(one_hot, jnp.concatenate(split3(values), axis=1).astype(BF16))
    return (parts[:, 0:width] + parts[:, width : 2 * width]) + parts[:, 2 * width :]


def pick_kernel(chosen, partials, norm, motions, tiles_out, edge_ref):
    motion = motions[4:8, :] + last_step(partials, norm) * motions[0:4, :]
    for edge in range(edge_ref.shape[0]):
        edge_ref[edge] = motion[:, edge * S : (edge + 1) * S]
    edges = [edge_ref[:, coordinate, :] for coordinate in range(3)]
    picked = choose(chosen[...], jnp.concatenate(edges + [jnp.zeros_like(edges[0])], axis=1))
    group, rows, _ = tiles_out.shape
    for place in range(group):
        tiles_out[place] = picked[place * rows : (place + 1) * rows, :]


def blend(index):
    fraction = index.astype(F32) / (S - 1)
    return 1.0 - fraction, fraction


def three_products(left, right):
    left_high, left_low = split2(left)
    right_high, right_low = split2(right)
    lefts = jnp.concatenate([left_high, left_high, left_low], axis=0)
    rights = jnp.concatenate([right_high, right_low, right_high], axis=0)
    return dot(lefts, rights, LEFT_T)


def block_kernel(placed, tiles, partials, norm, pair, out, coefficients_out, *scratch):
    tile_ref, spread_ref, weight_ref, held_ref, coefficients_ref, done, coefficients_done = scratch
    slots = out.shape[0]
    cells = S * S
    halves = done.shape[2]
    arrived = choose(placed[...], jnp.concatenate([tiles[source] for source in range(tiles.shape[0])], axis=0))
    for slot in range(slots):
        tile_ref[slot] = arrived[16 * slot : 16 * slot + 16, :]

    def copies(slot, coordinate):
        rows = S // halves
        return [
            pltpu.make_async_copy(
                held_ref.at[slot, coordinate, pl.ds(half * rows, rows), :],
                out.at[slot, coordinate, pl.ds(half * rows, rows), :],
                done.at[slot, coordinate, half],
            )
            for half in range(halves)
        ]

    index = lax.broadcasted_iota(jnp.int32, (S, 2 * S), 0)
    lane = lax.broadcasted_iota(jnp.int32, (S, 2 * S), 1)
    half = jnp.where(lane < S, 0, 1)
    third = jnp.where(index == lane - S * half, 1.0, 0.0).astype(BF16)
    for first in range(0, cells, 2 * S):
        columns = slice(first, first + 2 * S)
        spread_ref[0:S, columns] = jnp.where(index - first // S == half, 1.0, 0.0).astype(BF16)
        spread_ref[S : 2 * S, columns] = third
    row = lax.broadcasted_iota(jnp.int32, (8, cells), 0)
    cell = lax.broadcasted_iota(jnp.int32, (8, cells), 1)
    j_low, j_high = blend(cell >> SHIFTS)
    k_low, k_high = blend(cell & (S - 1))
    j_weight = jnp.where(row & 1 == 0, j_low, j_high)
    k_weight = jnp.where(row < 2, k_low, k_high)
    weight_ref[0] = jnp.where(row < 4, j_weight * k_weight, 0.0)
    lower = row & 2 == 0
    weight_ref[1] = jnp.where(row < 4, jnp.where(lower, k_low, k_high), jnp.where(lower, j_low, j_high))

    along_low, along_high = blend(lax.broadcasted_iota(jnp.int32, (8, S), 1))
    row = lax.broadcasted_iota(jnp.int32, (8, S), 0)
    side = jnp.where(row & 1 == 0, along_low, along_high)

    def fill(slot, carry):
        for coordinate in range(3):
            tile = tile_ref[slot][:, coordinate * S : (coordinate + 1) * S]
            first, others = tile[0:8], tile[8:16]
            straight = along_low * first[:, 0:1] + along_high * first[:, S - 1 : S]
            bent = jnp.where(row < 4, first - 2.0 * straight, 0.0)
            zero = jnp.zeros_like(others)
            placed = jnp.concatenate([jnp.where(row < 4, others, zero), jnp.where(row < 4, zero, others)], axis=1)
            spread = end_sum(dot(jnp.concatenate(split2(placed), axis=0), spread_ref[...]))
            lefts = jnp.concatenate([bent, side], axis=0)
            rights = jnp.concatenate([weight_ref[0], spread * weight_ref[1]], axis=0)
            held_ref[slot, coordinate] = three_products(lefts, rights)
            for copy in copies(slot, coordinate):
                copy.start()
        return carry

    lax.fori_loop(0, slots, fill, 0)
    mine = own_part(pair, own_index(), coefficients_out.shape[1])
    coefficients_ref[...] = (mine[4:8] + last_step(partials, norm) * mine[0:4])[0:3]
    last_copy = pltpu.make_async_copy(coefficients_ref, coefficients_out, coefficients_done)
    last_copy.start()
    for slot in range(slots):
        for coordinate in range(3):
            for copy in copies(slot, coordinate):
                copy.wait()
    last_copy.wait()


def call(kernel, name, outs, specs, scratch=(), megabytes=13, **more):
    shapes = tuple(jax.ShapeDtypeStruct(shape, dtype) for shape, dtype in outs)
    return pl.pallas_call(
        kernel,
        out_shape=shapes,
        in_specs=specs,
        scratch_shapes=scratch,
        compiler_params=pltpu.CompilerParams(vmem_limit_bytes=megabytes << 20),
        cost_estimate=pl.CostEstimate(flops=1, bytes_accessed=1, transcendentals=0),
        name=name,
        **{"out_specs": tuple(VMEM for _ in shapes), **more},
    )


def shards(total, center_points, displacements, edge_points, send_list, block_tiles, block_count):
    width = center_points.shape[1]
    extent = total * width
    edge_width = edge_points.shape[1]
    group, capacity = send_list.shape[1:]
    slots = block_tiles.shape[0]
    rows = -(-capacity // 8) * 8
    wanted = jnp.pad(send_list[0], ((0, 0), (0, rows - capacity)), constant_values=-1).reshape(group * rows, 1)
    chosen = (wanted == jnp.arange(edge_width // S)[None, :]).astype(BF16)
    tile_rows = block_tiles // capacity * rows + block_tiles % capacity
    tile_rows = jnp.where(jnp.arange(slots)[:, None] < block_count[0], tile_rows, -1)
    empty = jnp.full((slots, 4), -1, tile_rows.dtype)
    tile_rows = jnp.concatenate([tile_rows[:, 0:4], empty, tile_rows[:, 4:12]], axis=1).reshape(slots * 16, 1)
    placed = (tile_rows == jnp.arange(group * rows)[None, :]).astype(BF16)

    def spread_out(copies, axes):
        return lax.all_to_all(copies, axes, split_axis=0, concat_axis=0, tiled=True)

    (packed,) = call(
        pack_kernel,
        "pack",
        [((total, 1, 6 * width), F32)],
        [VMEM],
    )(jnp.concatenate([displacements, center_points], axis=0))
    packed = spread_out(packed, BOTH)
    matrix = ((extent, width), BF16)
    thin = ((total, 1, 3 * width), F32)
    size = math.gcd(extent, 512)
    kept = pltpu.VMEM((extent // size, 16, size), BF16)
    every, right, high, low, applied = call(
        build_kernel,
        "build",
        [((8, extent), F32), ((extent, 48), BF16), matrix, matrix, thin],
        [VMEM, ANY, ANY],
        [pltpu.VMEM((48, width), BF16), kept],
    )(packed, chosen, placed)
    applied = spread_out(applied, BOTH)
    applied, search, remain, numbers = call(
        turn_one_kernel,
        "turn_one",
        [thin, ((4, extent), F32), ((4, extent), F32), ((2, 4, 128), F32)],
        [VMEM] * 4,
    )(every, applied, high, low)
    applied = spread_out(applied, BOTH)
    partials, pair, norm = call(
        turn_two_kernel,
        "turn_two",
        [((total, 1, 128), F32), ((8, extent), F32), ((4, 128), F32)],
        [VMEM] * 7,
    )(every, applied, search, remain, numbers, high, low)
    partials = spread_out(partials, BOTH)
    (motions,) = call(
        edge_kernel,
        "edges",
        [((8, edge_width), F32)],
        [VMEM] * 3,
        [pltpu.VMEM((48, edge_width), BF16), pltpu.VMEM((8, edge_width), F32), kept],
    )(right, edge_points, pair)
    (tiles,) = call(
        pick_kernel,
        "pick",
        [((group, rows, 4 * S), F32)],
        [VMEM] * 4,
        [pltpu.VMEM((edge_width // S, 4, S), F32)],
    )(chosen, partials, norm, motions)
    tiles = spread_out(tiles, "gy")
    block_motion, coefficients = call(
        block_kernel,
        "blocks",
        [((slots, 3, S, S * S), F32), ((3, width), F32)],
        [VMEM] * 5,
        [
            pltpu.VMEM((slots, 16, 4 * S), F32),
            pltpu.VMEM((2 * S, S * S), BF16),
            pltpu.VMEM((2, 8, S * S), F32),
            pltpu.VMEM((slots, 3, S, S * S), F32),
            pltpu.VMEM((3, width), F32),
            pltpu.SemaphoreType.DMA((slots, 3, 2)),
            pltpu.SemaphoreType.DMA,
        ],
        24,
        out_specs=(ANY, ANY),
    )(placed, tiles, partials, norm, pair)
    return coefficients, block_motion


def solution(mesh):
    total = mesh.shape["gx"] * mesh.shape["gy"]
    split = P(None, BOTH)
    return jax.shard_map(
        functools.partial(shards, total),
        mesh=mesh,
        in_specs=(split, split, split, P(BOTH, None, None), P(BOTH, None), P(BOTH)),
        out_specs=(split, P(BOTH, None, None, None)),
        check_vma=False,
    )
```

```python
import functools
import math

import jax
import jax.numpy as jnp
from jax import lax
from jax.experimental import pallas as pl
from jax.experimental.pallas import tpu as pltpu
from jax.sharding import PartitionSpec as P

S = 64
SHIFTS = S.bit_length() - 1
SHIFT = 0.1
INV_RADIUS = 4.0
TINY = 1e-12
BOTH = ("gx", "gy")
F32, BF16 = jnp.float32, jnp.bfloat16
ANY = pl.BlockSpec(memory_space=pl.ANY)
VMEM = pl.BlockSpec(memory_space=pltpu.VMEM)
PLAIN = (((1,), (0,)), ((), ()))
LEFT_T = (((0,), (0,)), ((), ()))


def dot(left, right, dims=PLAIN):
    return lax.dot_general(left, right, dims, preferred_element_type=F32)


def split2(value):
    high = value.astype(BF16)
    return high, (value - high.astype(F32)).astype(BF16)


def split3(value):
    high = value.astype(BF16).astype(F32)
    rest = value - high
    middle = rest.astype(BF16).astype(F32)
    return high, middle, rest - middle


def features(points, is_left):
    row = lax.broadcasted_iota(jnp.int32, points.shape, 0)
    is_point = (row >= 4) & (row < 7)
    scaled = jnp.where(is_point, (points - 0.5) * INV_RADIUS, 0.0)
    norm = jnp.sum(scaled * scaled, axis=0, keepdims=True)
    own_row, other_row = (0, 1) if is_left else (1, 0)
    if is_left:
        scaled = -2.0 * scaled
    high, middle, low = split3(scaled)

    def with_norm(part, norm_part):
        return jnp.where(row == own_row, norm_part, jnp.where(row == other_row, 1.0, part))

    norms = split3(norm)
    if is_left:
        parts = [with_norm(high, n) for n in norms] + [middle, middle, low]
    else:
        parts = [with_norm(p, n) for p, n in zip((high, middle, low), norms)] + [high, middle, high]
    return jnp.concatenate(parts, axis=0).astype(BF16)


def quarter_phi(squared):
    squared = jnp.maximum(squared, TINY)
    radial = pltpu.reciprocal(lax.rsqrt(squared), approx=True)
    remain = jnp.maximum(1.0 - radial, 0.0)
    remain2 = remain * remain
    return (remain2 * remain2) * (1.25 - remain)


def write_copies(rows, out, first=0):
    width = rows.shape[1]
    for number in range(3):
        place = (first + number) * width
        out[:, :, place : place + width] = jnp.broadcast_to(rows[number : number + 1][None], (out.shape[0], 1, width))


def read_copies(ref, parts, width, first=0):
    lanes = ref.shape[-1]
    pieces = []
    for part in range(parts):
        if width % 128:
            start = first * width
            row = ref[part]
            values = [row[:, start + number * width : start + (number + 1) * width] for number in range(3)]
            pieces.append(jnp.concatenate(values, axis=0))
            continue
        step = width // lanes
        for piece in range(step):
            start = part * (ref.shape[0] // parts) + first * step + piece
            pieces.append(ref[pl.ds(start, 3, stride=step), :])
    rows = jnp.concatenate(pieces, axis=1)
    return jnp.concatenate([rows, jnp.zeros_like(rows[0:1])], axis=0)


def pack_kernel(stacked, out):
    write_copies(stacked[0:3, :], out)
    write_copies(stacked[3:6, :], out, 3)


def own_index():
    return lax.axis_index("gx") * lax.axis_size("gy") + lax.axis_index("gy")


def whole_slice(number, size):
    return pl.ds(pl.multiple_of(number * size, size), size)


def keep_vector(vector, kept_ref):
    both = jnp.concatenate(split2(4.0 * vector), axis=0)
    points = kept_ref.shape[2]
    for number in range(kept_ref.shape[0]):
        kept_ref[number] = both[:, number * points : (number + 1) * points]


def end_sum(both):
    rows = both.shape[0] // 2
    return both[:rows] + both[rows:]


def made_product(right_ref, left_ref, kept_ref, inside, store=None):
    pieces, rows, size = kept_ref.shape
    width = left_ref.shape[1]
    step_columns = math.gcd(width, 256)
    columns = [slice(first, first + step_columns) for first in range(0, width, step_columns)]
    inside = math.gcd(pieces, inside)

    def one_round(turn, sums):
        sums = list(sums)
        for step in range(inside):
            number = turn * inside + step
            for place, piece in enumerate(columns):
                squared = dot(right_ref[whole_slice(number, size), :], left_ref[:, piece])
                weights = split2(quarter_phi(squared))
                if store is not None:
                    for held, part in zip(store, weights):
                        held[whole_slice(number, size), piece] = part
                for part in weights:
                    sums[place] += dot(kept_ref[number], part)
        return tuple(sums)

    start = tuple(jnp.zeros((rows, step_columns), F32) for _ in columns)
    sums = lax.fori_loop(0, pieces // inside, one_round, start)
    return [(piece, end_sum(both)) for piece, both in zip(columns, sums)]


def kept_product(vector, high_ref, low_ref):
    both = jnp.concatenate(split2(4.0 * vector), axis=0)
    return end_sum(dot(both, high_ref[...]) + dot(both, low_ref[...]))


def build_kernel(packed, chosen, placed, every_out, right_ref, high_ref, low_ref, applied_out, left_ref, kept_ref):
    width = left_ref.shape[1]
    parts = right_ref.shape[0] // width
    shifts = read_copies(packed, parts, width)
    centers = read_copies(packed, parts, width, 3)
    every_out[0:4, :] = shifts
    every_out[4:8, :] = centers
    mine = own_part(every_out, own_index(), width)
    left_ref[...] = features(mine, True)
    right_ref[...] = features(every_out[...], False).T
    keep_vector(jnp.concatenate([shifts, jnp.zeros_like(shifts)], axis=0), kept_ref)
    ((_, product),) = made_product(right_ref, left_ref, kept_ref, 8, (high_ref, low_ref))
    write_copies(product[0:4] + SHIFT * mine[0:4], applied_out)


def edge_kernel(right_ref, points, pair, out, left_ref, padded_ref, kept_ref):
    padded_ref[...] = jnp.zeros_like(padded_ref)
    padded_ref[4:7, :] = points[...]
    left_ref[...] = features(padded_ref[...], True)
    keep_vector(pair[...], kept_ref)
    for piece, product in made_product(right_ref, left_ref, kept_ref, 8):
        out[:, piece] = product


def lane_sum(value):
    return jnp.sum(value, axis=1, keepdims=True)


def ratio(top, bottom):
    row = lax.broadcasted_iota(jnp.int32, top.shape, 0)
    return jnp.where(row < 3, top / jnp.where(row < 3, bottom, 1.0), 0.0)


def own_part(ref, me, width):
    if width % 128 == 0:
        return ref[:, pl.ds(pl.multiple_of(me * width, 128), width)]
    lane = lax.broadcasted_iota(jnp.int32, (ref.shape[1], width), 0)
    column = lax.broadcasted_iota(jnp.int32, (ref.shape[1], width), 1)
    chosen = jnp.where(lane == me * width + column, 1.0, 0.0)
    return lax.dot_general(ref[...], chosen, PLAIN, precision=lax.Precision.HIGHEST, preferred_element_type=F32)


def turn_one_kernel(every, applied, high_ref, low_ref, applied_out, search_out, remain_out, numbers_out):
    width = high_ref.shape[1]
    start = every[0:4, :]
    got = read_copies(applied, every.shape[1] // width, width)
    norm = lane_sum(start * start)
    step = ratio(norm, lane_sum(start * got))
    remain = start - step * got
    following = lane_sum(remain * remain)
    search = remain + ratio(following, norm) * start
    search_out[...] = search
    remain_out[...] = remain
    numbers_out[0] = jnp.broadcast_to(step, numbers_out.shape[1:])
    numbers_out[1] = jnp.broadcast_to(following, numbers_out.shape[1:])
    product = kept_product(jnp.concatenate([search, jnp.zeros_like(search)], axis=0), high_ref, low_ref)
    write_copies(product[0:4] + SHIFT * own_part(search_out, own_index(), width), applied_out)


def turn_two_kernel(every, applied, search_in, remain_in, numbers, high_ref, low_ref, partial_out, pair_out, norm_out):
    width = high_ref.shape[1]
    start = every[0:4, :]
    got = read_copies(applied, every.shape[1] // width, width)
    search = search_in[...]
    norm = numbers[1][:, 0:1]
    step = ratio(norm, lane_sum(search * got))
    iterate = numbers[0][:, 0:1] * start + step * search
    remain = remain_in[...] - step * got
    following = lane_sum(remain * remain)
    search = remain + ratio(following, norm) * search
    pair = jnp.concatenate([search, iterate], axis=0)
    pair_out[...] = pair
    norm_out[...] = jnp.broadcast_to(following, norm_out.shape)
    product = kept_product(pair, high_ref, low_ref)
    mine = own_part(pair_out, own_index(), width)[0:4]
    product = product[0:4] + SHIFT * mine
    partial = lane_sum(mine * product)
    lane = lax.broadcasted_iota(jnp.int32, (1, partial_out.shape[2]), 1)
    row = jnp.zeros(lane.shape, F32)
    for number in range(3):
        row = jnp.where(lane == number, partial[number : number + 1], row)
    partial_out[...] = jnp.broadcast_to(row[None], partial_out.shape)


def last_step(partials, norm):
    row = jnp.sum(partials[...], axis=0)
    number = lax.broadcasted_iota(jnp.int32, (4, 1), 0)
    total = jnp.ones((4, 1), F32)
    for coordinate in range(3):
        total = jnp.where(number == coordinate, row[:, coordinate : coordinate + 1], total)
    return ratio(norm[:, 0:1], total)


def choose(one_hot, values):
    width = values.shape[1]
    parts = dot(one_hot, jnp.concatenate(split3(values), axis=1).astype(BF16))
    return (parts[:, 0:width] + parts[:, width : 2 * width]) + parts[:, 2 * width :]


def pick_kernel(chosen, partials, norm, motions, tiles_out, edge_ref):
    motion = motions[4:8, :] + last_step(partials, norm) * motions[0:4, :]
    for edge in range(edge_ref.shape[0]):
        edge_ref[edge] = motion[:, edge * S : (edge + 1) * S]
    edges = [edge_ref[:, coordinate, :] for coordinate in range(3)]
    picked = choose(chosen[...], jnp.concatenate(edges + [jnp.zeros_like(edges[0])], axis=1))
    group, rows, _ = tiles_out.shape
    for place in range(group):
        tiles_out[place] = picked[place * rows : (place + 1) * rows, :]


def blend(index):
    fraction = index.astype(F32) / (S - 1)
    return 1.0 - fraction, fraction


def three_products(left, right):
    left_high, left_low = split2(left)
    right_high, right_low = split2(right)
    lefts = jnp.concatenate([left_high, left_high, left_low], axis=0)
    rights = jnp.concatenate([right_high, right_low, right_high], axis=0)
    return dot(lefts, rights, LEFT_T)


def block_kernel(placed, tiles, partials, norm, pair, out, coefficients_out, *scratch):
    tile_ref, spread_ref, weight_ref, held_ref, coefficients_ref, done, coefficients_done = scratch
    slots = out.shape[0]
    cells = S * S
    halves = done.shape[2]
    arrived = choose(placed[...], jnp.concatenate([tiles[source] for source in range(tiles.shape[0])], axis=0))
    for slot in range(slots):
        tile_ref[slot] = arrived[16 * slot : 16 * slot + 16, :]

    def copies(slot, coordinate):
        rows = S // halves
        return [
            pltpu.make_async_copy(
                held_ref.at[slot, coordinate, pl.ds(half * rows, rows), :],
                out.at[slot, coordinate, pl.ds(half * rows, rows), :],
                done.at[slot, coordinate, half],
            )
            for half in range(halves)
        ]

    index = lax.broadcasted_iota(jnp.int32, (S, 2 * S), 0)
    lane = lax.broadcasted_iota(jnp.int32, (S, 2 * S), 1)
    half = jnp.where(lane < S, 0, 1)
    third = jnp.where(index == lane - S * half, 1.0, 0.0).astype(BF16)
    for first in range(0, cells, 2 * S):
        columns = slice(first, first + 2 * S)
        spread_ref[0:S, columns] = jnp.where(index - first // S == half, 1.0, 0.0).astype(BF16)
        spread_ref[S : 2 * S, columns] = third
    row = lax.broadcasted_iota(jnp.int32, (8, cells), 0)
    cell = lax.broadcasted_iota(jnp.int32, (8, cells), 1)
    j_low, j_high = blend(cell >> SHIFTS)
    k_low, k_high = blend(cell & (S - 1))
    j_weight = jnp.where(row & 1 == 0, j_low, j_high)
    k_weight = jnp.where(row < 2, k_low, k_high)
    weight_ref[0] = jnp.where(row < 4, j_weight * k_weight, 0.0)
    lower = row & 2 == 0
    weight_ref[1] = jnp.where(row < 4, jnp.where(lower, k_low, k_high), jnp.where(lower, j_low, j_high))

    along_low, along_high = blend(lax.broadcasted_iota(jnp.int32, (8, S), 1))
    row = lax.broadcasted_iota(jnp.int32, (8, S), 0)
    side = jnp.where(row & 1 == 0, along_low, along_high)

    def fill(slot, carry):
        for coordinate in range(3):
            tile = tile_ref[slot][:, coordinate * S : (coordinate + 1) * S]
            first, others = tile[0:8], tile[8:16]
            straight = along_low * first[:, 0:1] + along_high * first[:, S - 1 : S]
            bent = jnp.where(row < 4, first - 2.0 * straight, 0.0)
            zero = jnp.zeros_like(others)
            placed = jnp.concatenate([jnp.where(row < 4, others, zero), jnp.where(row < 4, zero, others)], axis=1)
            spread = end_sum(dot(jnp.concatenate(split2(placed), axis=0), spread_ref[...]))
            lefts = jnp.concatenate([bent, side], axis=0)
            rights = jnp.concatenate([weight_ref[0], spread * weight_ref[1]], axis=0)
            held_ref[slot, coordinate] = three_products(lefts, rights)
            for copy in copies(slot, coordinate):
                copy.start()
        return carry

    lax.fori_loop(0, slots, fill, 0)
    mine = own_part(pair, own_index(), coefficients_out.shape[1])
    coefficients_ref[...] = (mine[4:8] + last_step(partials, norm) * mine[0:4])[0:3]
    last_copy = pltpu.make_async_copy(coefficients_ref, coefficients_out, coefficients_done)
    last_copy.start()
    for slot in range(slots):
        for coordinate in range(3):
            for copy in copies(slot, coordinate):
                copy.wait()
    last_copy.wait()


def call(kernel, name, outs, specs, scratch=(), megabytes=13, **more):
    shapes = tuple(jax.ShapeDtypeStruct(shape, dtype) for shape, dtype in outs)
    return pl.pallas_call(
        kernel,
        out_shape=shapes,
        in_specs=specs,
        scratch_shapes=scratch,
        compiler_params=pltpu.CompilerParams(vmem_limit_bytes=megabytes << 20),
        cost_estimate=pl.CostEstimate(flops=1, bytes_accessed=1, transcendentals=0),
        name=name,
        **{"out_specs": tuple(VMEM for _ in shapes), **more},
    )


def shards(total, center_points, displacements, edge_points, send_list, block_tiles, block_count):
    width = center_points.shape[1]
    extent = total * width
    edge_width = edge_points.shape[1]
    group, capacity = send_list.shape[1:]
    slots = block_tiles.shape[0]
    rows = -(-capacity // 8) * 8
    wanted = jnp.pad(send_list[0], ((0, 0), (0, rows - capacity)), constant_values=-1).reshape(group * rows, 1)
    chosen = (wanted == jnp.arange(edge_width // S)[None, :]).astype(BF16)
    tile_rows = block_tiles // capacity * rows + block_tiles % capacity
    tile_rows = jnp.where(jnp.arange(slots)[:, None] < block_count[0], tile_rows, -1)
    empty = jnp.full((slots, 4), -1, tile_rows.dtype)
    tile_rows = jnp.concatenate([tile_rows[:, 0:4], empty, tile_rows[:, 4:12]], axis=1).reshape(slots * 16, 1)
    placed = (tile_rows == jnp.arange(group * rows)[None, :]).astype(BF16)

    def spread_out(copies, axes):
        return lax.all_to_all(copies, axes, split_axis=0, concat_axis=0, tiled=True)

    def rows_of(array):
        return array if width % 128 else array.reshape(-1, 128)

    (packed,) = call(
        pack_kernel,
        "pack",
        [((total, 1, 6 * width), F32)],
        [VMEM],
    )(jnp.concatenate([displacements, center_points], axis=0))
    packed = rows_of(spread_out(packed, BOTH))
    matrix = ((extent, width), BF16)
    thin = ((total, 1, 3 * width), F32)
    size = math.gcd(extent, 512)
    kept = pltpu.VMEM((extent // size, 16, size), BF16)
    every, right, high, low, applied = call(
        build_kernel,
        "build",
        [((8, extent), F32), ((extent, 48), BF16), matrix, matrix, thin],
        [VMEM, ANY, ANY],
        [pltpu.VMEM((48, width), BF16), kept],
    )(packed, chosen, placed)
    applied = rows_of(spread_out(applied, BOTH))
    applied, search, remain, numbers = call(
        turn_one_kernel,
        "turn_one",
        [thin, ((4, extent), F32), ((4, extent), F32), ((2, 4, 128), F32)],
        [VMEM] * 4,
    )(every, applied, high, low)
    applied = rows_of(spread_out(applied, BOTH))
    partials, pair, norm = call(
        turn_two_kernel,
        "turn_two",
        [((total, 1, 128), F32), ((8, extent), F32), ((4, 128), F32)],
        [VMEM] * 7,
    )(every, applied, search, remain, numbers, high, low)
    partials = spread_out(partials, BOTH)
    (motions,) = call(
        edge_kernel,
        "edges",
        [((8, edge_width), F32)],
        [VMEM] * 3,
        [pltpu.VMEM((48, edge_width), BF16), pltpu.VMEM((8, edge_width), F32), kept],
    )(right, edge_points, pair)
    (tiles,) = call(
        pick_kernel,
        "pick",
        [((group, rows, 4 * S), F32)],
        [VMEM] * 4,
        [pltpu.VMEM((edge_width // S, 4, S), F32)],
    )(chosen, partials, norm, motions)
    tiles = spread_out(tiles, "gy")
    block_motion, coefficients = call(
        block_kernel,
        "blocks",
        [((slots, 3, S, S * S), F32), ((3, width), F32)],
        [VMEM] * 5,
        [
            pltpu.VMEM((slots, 16, 4 * S), F32),
            pltpu.VMEM((2 * S, S * S), BF16),
            pltpu.VMEM((2, 8, S * S), F32),
            pltpu.VMEM((slots, 3, S, S * S), F32),
            pltpu.VMEM((3, width), F32),
            pltpu.SemaphoreType.DMA((slots, 3, 2)),
            pltpu.SemaphoreType.DMA,
        ],
        24,
        out_specs=(ANY, ANY),
    )(placed, tiles, partials, norm, pair)
    return coefficients, block_motion


def solution(mesh):
    total = mesh.shape["gx"] * mesh.shape["gy"]
    split = P(None, BOTH)
    return jax.shard_map(
        functools.partial(shards, total),
        mesh=mesh,
        in_specs=(split, split, split, P(BOTH, None, None), P(BOTH, None), P(BOTH)),
        out_specs=(split, P(BOTH, None, None, None)),
        check_vma=False,
    )
```

```python
import functools
import math

import jax
import jax.numpy as jnp
from jax import lax
from jax.experimental import pallas as pl
from jax.experimental.pallas import tpu as pltpu
from jax.sharding import PartitionSpec as P

S = 64
SHIFTS = S.bit_length() - 1
SHIFT = 0.1
INV_RADIUS = 4.0
TINY = 1e-12
BOTH = ("gx", "gy")
F32, BF16 = jnp.float32, jnp.bfloat16
ANY = pl.BlockSpec(memory_space=pl.ANY)
VMEM = pl.BlockSpec(memory_space=pltpu.VMEM)
PLAIN = (((1,), (0,)), ((), ()))
LEFT_T = (((0,), (0,)), ((), ()))


def dot(left, right, dims=PLAIN):
    return lax.dot_general(left, right, dims, preferred_element_type=F32)


def split2(value):
    high = value.astype(BF16)
    return high, (value - high.astype(F32)).astype(BF16)


def split3(value):
    high = value.astype(BF16).astype(F32)
    rest = value - high
    middle = rest.astype(BF16).astype(F32)
    return high, middle, rest - middle


def features(points, is_left):
    row = lax.broadcasted_iota(jnp.int32, points.shape, 0)
    is_point = (row >= 4) & (row < 7)
    scaled = jnp.where(is_point, (points - 0.5) * INV_RADIUS, 0.0)
    norm = jnp.sum(scaled * scaled, axis=0, keepdims=True)
    own_row, other_row = (0, 1) if is_left else (1, 0)
    if is_left:
        scaled = -2.0 * scaled
    high, middle, low = split3(scaled)

    def with_norm(part, norm_part):
        return jnp.where(row == own_row, norm_part, jnp.where(row == other_row, 1.0, part))

    norms = split3(norm)
    if is_left:
        parts = [with_norm(high, n) for n in norms] + [middle, middle, low]
    else:
        parts = [with_norm(p, n) for p, n in zip((high, middle, low), norms)] + [high, middle, high]
    return jnp.concatenate(parts, axis=0).astype(BF16)


def quarter_phi(squared):
    squared = jnp.maximum(squared, TINY)
    radial = pltpu.reciprocal(lax.rsqrt(squared), approx=True)
    remain = jnp.maximum(1.0 - radial, 0.0)
    remain2 = remain * remain
    return (remain2 * remain2) * (1.25 - remain)


def write_copies(rows, out, first=0):
    width = rows.shape[1]
    for number in range(3):
        place = (first + number) * width
        out[:, :, place : place + width] = jnp.broadcast_to(rows[number : number + 1][None], (out.shape[0], 1, width))


def read_copies(ref, parts, width, first=0):
    lanes = ref.shape[-1]
    pieces = []
    for part in range(parts):
        if width % 128:
            start = first * width
            row = ref[part]
            values = [row[:, start + number * width : start + (number + 1) * width] for number in range(3)]
            pieces.append(jnp.concatenate(values, axis=0))
            continue
        step = width // lanes
        for piece in range(step):
            start = part * (ref.shape[0] // parts) + first * step + piece
            pieces.append(ref[pl.ds(start, 3, stride=step), :])
    rows = jnp.concatenate(pieces, axis=1)
    return jnp.concatenate([rows, jnp.zeros_like(rows[0:1])], axis=0)


def pack_kernel(stacked, out):
    write_copies(stacked[0:3, :], out)
    write_copies(stacked[3:6, :], out, 3)


def own_index():
    return lax.axis_index("gx") * lax.axis_size("gy") + lax.axis_index("gy")


def whole_slice(number, size):
    return pl.ds(pl.multiple_of(number * size, size), size)


def keep_vector(vector, kept_ref):
    both = jnp.concatenate(split2(4.0 * vector), axis=0)
    points = kept_ref.shape[2]
    for number in range(kept_ref.shape[0]):
        kept_ref[number] = both[:, number * points : (number + 1) * points]


def end_sum(both):
    rows = both.shape[0] // 2
    return both[:rows] + both[rows:]


def made_product(right_ref, left_ref, kept_ref, inside, store=None):
    pieces, rows, size = kept_ref.shape
    width = left_ref.shape[1]
    step_columns = math.gcd(width, 256)
    columns = [slice(first, first + step_columns) for first in range(0, width, step_columns)]
    inside = math.gcd(pieces, inside)

    def one_round(turn, sums):
        sums = list(sums)
        for step in range(inside):
            number = turn * inside + step
            for place, piece in enumerate(columns):
                squared = dot(right_ref[whole_slice(number, size), :], left_ref[:, piece])
                weights = split2(quarter_phi(squared))
                if store is not None:
                    for held, part in zip(store, weights):
                        held[whole_slice(number, size), piece] = part
                for part in weights:
                    sums[place] += dot(kept_ref[number], part)
        return tuple(sums)

    start = tuple(jnp.zeros((rows, step_columns), F32) for _ in columns)
    sums = lax.fori_loop(0, pieces // inside, one_round, start)
    return [(piece, end_sum(both)) for piece, both in zip(columns, sums)]


def kept_product(vector, high_ref, low_ref):
    both = jnp.concatenate(split2(4.0 * vector), axis=0)
    return end_sum(dot(both, high_ref[...]) + dot(both, low_ref[...]))


def build_kernel(packed, chosen, placed, every_out, right_ref, high_ref, low_ref, applied_out, left_ref, kept_ref):
    width = left_ref.shape[1]
    parts = right_ref.shape[0] // width
    shifts = read_copies(packed, parts, width)
    centers = read_copies(packed, parts, width, 3)
    every_out[0:4, :] = shifts
    every_out[4:8, :] = centers
    mine = own_part(every_out, own_index(), width)
    left_ref[...] = features(mine, True)
    right_ref[...] = features(every_out[...], False).T
    keep_vector(jnp.concatenate([shifts, jnp.zeros_like(shifts)], axis=0), kept_ref)
    ((_, product),) = made_product(right_ref, left_ref, kept_ref, 8, (high_ref, low_ref))
    write_copies(product[0:4] + SHIFT * mine[0:4], applied_out)


def edge_kernel(right_ref, points, pair, out, left_ref, padded_ref, kept_ref):
    padded_ref[...] = jnp.zeros_like(padded_ref)
    padded_ref[4:7, :] = points[...]
    left_ref[...] = features(padded_ref[...], True)
    keep_vector(pair[...], kept_ref)
    for piece, product in made_product(right_ref, left_ref, kept_ref, 8):
        out[:, piece] = product


def lane_sum(value):
    return jnp.sum(value, axis=1, keepdims=True)


def ratio(top, bottom):
    row = lax.broadcasted_iota(jnp.int32, top.shape, 0)
    return jnp.where(row < 3, top / jnp.where(row < 3, bottom, 1.0), 0.0)


def own_part(ref, me, width):
    if width % 128 == 0:
        return ref[:, pl.ds(pl.multiple_of(me * width, 128), width)]
    lane = lax.broadcasted_iota(jnp.int32, (ref.shape[1], width), 0)
    column = lax.broadcasted_iota(jnp.int32, (ref.shape[1], width), 1)
    chosen = jnp.where(lane == me * width + column, 1.0, 0.0)
    return lax.dot_general(ref[...], chosen, PLAIN, precision=lax.Precision.HIGHEST, preferred_element_type=F32)


def turn_one_kernel(every, applied, high_ref, low_ref, applied_out, search_out, remain_out, numbers_out):
    width = high_ref.shape[1]
    start = every[0:4, :]
    got = read_copies(applied, every.shape[1] // width, width)
    norm = lane_sum(start * start)
    step = ratio(norm, lane_sum(start * got))
    remain = start - step * got
    following = lane_sum(remain * remain)
    search = remain + ratio(following, norm) * start
    search_out[...] = search
    remain_out[...] = remain
    numbers_out[0] = jnp.broadcast_to(step, numbers_out.shape[1:])
    numbers_out[1] = jnp.broadcast_to(following, numbers_out.shape[1:])
    product = kept_product(jnp.concatenate([search, jnp.zeros_like(search)], axis=0), high_ref, low_ref)
    write_copies(product[0:4] + SHIFT * own_part(search_out, own_index(), width), applied_out)


def turn_two_kernel(every, applied, search_in, remain_in, numbers, high_ref, low_ref, *rest):
    partial_out, pair_out, norm_out, partial_ref, done = rest
    width = high_ref.shape[1]
    got = read_copies(applied, every.shape[1] // width, width)
    search = search_in[...]
    norm = numbers[1][:, 0:1]
    step = ratio(norm, lane_sum(search * got))
    remain = remain_in[...] - step * got
    following = lane_sum(remain * remain)
    new_search = remain + ratio(following, norm) * search
    pair_out[0:4, :] = new_search
    product = kept_product(jnp.concatenate([new_search, jnp.zeros_like(new_search)], axis=0), high_ref, low_ref)
    mine = own_part(pair_out, own_index(), width)[0:4]
    partial = lane_sum(mine * (product[0:4] + SHIFT * mine))
    lane = lax.broadcasted_iota(jnp.int32, (1, partial_ref.shape[2]), 1)
    row = jnp.zeros(lane.shape, F32)
    for number in range(3):
        row = jnp.where(lane == number, partial[number : number + 1], row)
    partial_ref[...] = jnp.broadcast_to(row[None], partial_ref.shape)
    copy = pltpu.make_async_copy(partial_ref, partial_out, done)
    copy.start()
    pair_out[4:8, :] = numbers[0][:, 0:1] * every[0:4, :] + step * search
    norm_out[...] = jnp.broadcast_to(following, norm_out.shape)
    copy.wait()


def last_step(partials, norm):
    row = jnp.sum(partials[...], axis=0)
    number = lax.broadcasted_iota(jnp.int32, (4, 1), 0)
    total = jnp.ones((4, 1), F32)
    for coordinate in range(3):
        total = jnp.where(number == coordinate, row[:, coordinate : coordinate + 1], total)
    return ratio(norm[:, 0:1], total)


def choose(one_hot, values):
    width = values.shape[1]
    parts = dot(one_hot, jnp.concatenate(split3(values), axis=1).astype(BF16))
    return (parts[:, 0:width] + parts[:, width : 2 * width]) + parts[:, 2 * width :]


def pick_kernel(chosen, partials, norm, motions, tiles_out, edge_ref):
    motion = motions[4:8, :] + last_step(partials, norm) * motions[0:4, :]
    for edge in range(edge_ref.shape[0]):
        edge_ref[edge] = motion[:, edge * S : (edge + 1) * S]
    edges = [edge_ref[:, coordinate, :] for coordinate in range(3)]
    picked = choose(chosen[...], jnp.concatenate(edges + [jnp.zeros_like(edges[0])], axis=1))
    group, rows, _ = tiles_out.shape
    for place in range(group):
        tiles_out[place] = picked[place * rows : (place + 1) * rows, :]


def blend(index):
    fraction = index.astype(F32) / (S - 1)
    return 1.0 - fraction, fraction


def three_products(left, right):
    left_high, left_low = split2(left)
    right_high, right_low = split2(right)
    lefts = jnp.concatenate([left_high, left_high, left_low], axis=0)
    rights = jnp.concatenate([right_high, right_low, right_high], axis=0)
    return dot(lefts, rights, LEFT_T)


def block_kernel(placed, tiles, partials, norm, pair, out, coefficients_out, *scratch):
    tile_ref, spread_ref, weight_ref, held_ref, coefficients_ref, done, coefficients_done = scratch
    slots = out.shape[0]
    cells = S * S
    halves = done.shape[2]
    arrived = choose(placed[...], jnp.concatenate([tiles[source] for source in range(tiles.shape[0])], axis=0))
    for slot in range(slots):
        tile_ref[slot] = arrived[16 * slot : 16 * slot + 16, :]

    def copies(slot, coordinate):
        rows = S // halves
        return [
            pltpu.make_async_copy(
                held_ref.at[slot, coordinate, pl.ds(half * rows, rows), :],
                out.at[slot, coordinate, pl.ds(half * rows, rows), :],
                done.at[slot, coordinate, half],
            )
            for half in range(halves)
        ]

    index = lax.broadcasted_iota(jnp.int32, (S, 2 * S), 0)
    lane = lax.broadcasted_iota(jnp.int32, (S, 2 * S), 1)
    half = jnp.where(lane < S, 0, 1)
    third = jnp.where(index == lane - S * half, 1.0, 0.0).astype(BF16)
    for first in range(0, cells, 2 * S):
        columns = slice(first, first + 2 * S)
        spread_ref[0:S, columns] = jnp.where(index - first // S == half, 1.0, 0.0).astype(BF16)
        spread_ref[S : 2 * S, columns] = third
    row = lax.broadcasted_iota(jnp.int32, (8, cells), 0)
    cell = lax.broadcasted_iota(jnp.int32, (8, cells), 1)
    j_low, j_high = blend(cell >> SHIFTS)
    k_low, k_high = blend(cell & (S - 1))
    j_weight = jnp.where(row & 1 == 0, j_low, j_high)
    k_weight = jnp.where(row < 2, k_low, k_high)
    weight_ref[0] = jnp.where(row < 4, j_weight * k_weight, 0.0)
    lower = row & 2 == 0
    weight_ref[1] = jnp.where(row < 4, jnp.where(lower, k_low, k_high), jnp.where(lower, j_low, j_high))

    along_low, along_high = blend(lax.broadcasted_iota(jnp.int32, (8, S), 1))
    row = lax.broadcasted_iota(jnp.int32, (8, S), 0)
    side = jnp.where(row & 1 == 0, along_low, along_high)

    def fill(slot, carry):
        for coordinate in range(3):
            tile = tile_ref[slot][:, coordinate * S : (coordinate + 1) * S]
            first, others = tile[0:8], tile[8:16]
            straight = along_low * first[:, 0:1] + along_high * first[:, S - 1 : S]
            bent = jnp.where(row < 4, first - 2.0 * straight, 0.0)
            zero = jnp.zeros_like(others)
            placed = jnp.concatenate([jnp.where(row < 4, others, zero), jnp.where(row < 4, zero, others)], axis=1)
            spread = end_sum(dot(jnp.concatenate(split2(placed), axis=0), spread_ref[...]))
            lefts = jnp.concatenate([bent, side], axis=0)
            rights = jnp.concatenate([weight_ref[0], spread * weight_ref[1]], axis=0)
            held_ref[slot, coordinate] = three_products(lefts, rights)
            for copy in copies(slot, coordinate):
                copy.start()
        return carry

    lax.fori_loop(0, slots, fill, 0)
    mine = own_part(pair, own_index(), coefficients_out.shape[1])
    coefficients_ref[...] = (mine[4:8] + last_step(partials, norm) * mine[0:4])[0:3]
    last_copy = pltpu.make_async_copy(coefficients_ref, coefficients_out, coefficients_done)
    last_copy.start()
    for slot in range(slots):
        for coordinate in range(3):
            for copy in copies(slot, coordinate):
                copy.wait()
    last_copy.wait()


def call(kernel, name, outs, specs, scratch=(), megabytes=13, **more):
    shapes = tuple(jax.ShapeDtypeStruct(shape, dtype) for shape, dtype in outs)
    return pl.pallas_call(
        kernel,
        out_shape=shapes,
        in_specs=specs,
        scratch_shapes=scratch,
        compiler_params=pltpu.CompilerParams(vmem_limit_bytes=megabytes << 20),
        cost_estimate=pl.CostEstimate(flops=1, bytes_accessed=1, transcendentals=0),
        name=name,
        **{"out_specs": tuple(VMEM for _ in shapes), **more},
    )


def shards(total, center_points, displacements, edge_points, send_list, block_tiles, block_count):
    width = center_points.shape[1]
    extent = total * width
    edge_width = edge_points.shape[1]
    group, capacity = send_list.shape[1:]
    slots = block_tiles.shape[0]
    rows = -(-capacity // 8) * 8
    wanted = jnp.pad(send_list[0], ((0, 0), (0, rows - capacity)), constant_values=-1).reshape(group * rows, 1)
    chosen = (wanted == jnp.arange(edge_width // S)[None, :]).astype(BF16)
    tile_rows = block_tiles // capacity * rows + block_tiles % capacity
    tile_rows = jnp.where(jnp.arange(slots)[:, None] < block_count[0], tile_rows, -1)
    empty = jnp.full((slots, 4), -1, tile_rows.dtype)
    tile_rows = jnp.concatenate([tile_rows[:, 0:4], empty, tile_rows[:, 4:12]], axis=1).reshape(slots * 16, 1)
    placed = (tile_rows == jnp.arange(group * rows)[None, :]).astype(BF16)

    def spread_out(copies, axes):
        return lax.all_to_all(copies, axes, split_axis=0, concat_axis=0, tiled=True)

    def rows_of(array):
        return array if width % 128 else array.reshape(-1, 128)

    (packed,) = call(
        pack_kernel,
        "pack",
        [((total, 1, 6 * width), F32)],
        [VMEM],
    )(jnp.concatenate([displacements, center_points], axis=0))
    packed = rows_of(spread_out(packed, BOTH))
    matrix = ((extent, width), BF16)
    thin = ((total, 1, 3 * width), F32)
    size = math.gcd(extent, 512)
    kept = pltpu.VMEM((extent // size, 16, size), BF16)
    every, right, high, low, applied = call(
        build_kernel,
        "build",
        [((8, extent), F32), ((extent, 48), BF16), matrix, matrix, thin],
        [VMEM, ANY, ANY],
        [pltpu.VMEM((48, width), BF16), kept],
    )(packed, chosen, placed)
    applied = rows_of(spread_out(applied, BOTH))
    applied, search, remain, numbers = call(
        turn_one_kernel,
        "turn_one",
        [thin, ((4, extent), F32), ((4, extent), F32), ((2, 4, 128), F32)],
        [VMEM] * 4,
    )(every, applied, high, low)
    applied = rows_of(spread_out(applied, BOTH))
    partials, pair, norm = call(
        turn_two_kernel,
        "turn_two",
        [((total, 1, 128), F32), ((8, extent), F32), ((4, 128), F32)],
        [VMEM] * 7,
        [pltpu.VMEM((total, 1, 128), F32), pltpu.SemaphoreType.DMA],
        out_specs=(ANY, VMEM, VMEM),
    )(every, applied, search, remain, numbers, high, low)
    partials = spread_out(partials, BOTH)
    (motions,) = call(
        edge_kernel,
        "edges",
        [((8, edge_width), F32)],
        [VMEM] * 3,
        [pltpu.VMEM((48, edge_width), BF16), pltpu.VMEM((8, edge_width), F32), kept],
    )(right, edge_points, pair)
    (tiles,) = call(
        pick_kernel,
        "pick",
        [((group, rows, 4 * S), F32)],
        [VMEM] * 4,
        [pltpu.VMEM((edge_width // S, 4, S), F32)],
    )(chosen, partials, norm, motions)
    tiles = spread_out(tiles, "gy")
    block_motion, coefficients = call(
        block_kernel,
        "blocks",
        [((slots, 3, S, S * S), F32), ((3, width), F32)],
        [VMEM] * 5,
        [
            pltpu.VMEM((slots, 16, 4 * S), F32),
            pltpu.VMEM((2 * S, S * S), BF16),
            pltpu.VMEM((2, 8, S * S), F32),
            pltpu.VMEM((slots, 3, S, S * S), F32),
            pltpu.VMEM((3, width), F32),
            pltpu.SemaphoreType.DMA((slots, 3, 1)),
            pltpu.SemaphoreType.DMA,
        ],
        24,
        out_specs=(ANY, ANY),
    )(placed, tiles, partials, norm, pair)
    return coefficients, block_motion


def solution(mesh):
    total = mesh.shape["gx"] * mesh.shape["gy"]
    split = P(None, BOTH)
    return jax.shard_map(
        functools.partial(shards, total),
        mesh=mesh,
        in_specs=(split, split, split, P(BOTH, None, None), P(BOTH, None), P(BOTH)),
        out_specs=(split, P(BOTH, None, None, None)),
        check_vma=False,
    )
```
